512 devices in a mesh: seq: 128 (over y_lo, x, z), chan: 4 (over y_hi, core).
Axes of the slice: x: 4, y: 8 (y_hi: 2, y_lo: 4; y = y_hi * 4 + y_lo), z: 8, core: 2. Of those that a mesh axis runs over, the one named last changes fastest.
Arguments:
- signal: bfloat16 [16, 1024, 1024], P('chan', 'seq'), may hold values from -24 to 24
- right_factor: bfloat16 [1024, 1024], P('chan'), may hold values from -0.1875 to 0.1875
- left_factor: bfloat16 [1024, 1024], P('chan'), may hold values from -0.1875 to 0.1875
- gate: bfloat16 [16, 1024, 1024], P('chan', 'seq'), may hold values from -6 to 6
- cotangent: bfloat16 [16, 1024, 1024], P('chan', 'seq'), may hold values from -1.5 to 1.5
Outputs:
- mixed: bfloat16 [16, 1024, 1024], P('chan', 'seq')
- right_grad: float32 [1024, 1024], P('chan', 'seq')
- left_grad: float32 [1024, 1024], P('chan', 'seq')
- gate_grad: bfloat16 [16, 1024, 1024], P('chan', 'seq')
- signal_grad: bfloat16 [16, 1024, 1024], P('chan', 'seq')
The draws below stay inside these ranges and needn't reach their ends.
All inputs are finite; a program needn't handle non-finite values.
Results may differ from the reference program's by a relative error of at most 0.0057.
Values may be sent and summed in bfloat16 or wider, within the bound.
No kernel may reach another device: no remote copies, remote signals or barrier semaphores. Data moves between devices by JAX's collectives and lax.ppermute only.
A program may use at most 64 MiB of HBM per device.

```python
import jax
import jax.numpy as jnp

B = 1024
CHANNELS = 16


def spiked(drawn, rng, source, target, shards_of, factor):
    owner, partner = [(jnp.arange(drawn.shape[position]) // (drawn.shape[position] // shards_of)).reshape([-1 if axis == position else 1 for axis in range(drawn.ndim)]) for position in (source, target)]
    chosen = jax.random.permutation(rng, shards_of)[partner]
    strong = (owner == chosen) | (owner == (partner + shards_of // 2) % shards_of)
    return jnp.where(strong, factor * drawn, drawn)


def levels(own_key, extent, cuts, smallest, high):
    level = 1.0
    for dim, parts in cuts:
        steps = jax.random.uniform(jax.random.fold_in(jax.random.fold_in(own_key, 6), dim), (parts,), jnp.float32, smallest / len(cuts), high / len(cuts))
        level = level * jnp.repeat(jnp.exp(steps), extent[dim] // parts).reshape((-1,) + (1,) * (len(extent) - 1 - dim))
    return level


def normal_values(stream_key, dims, scale, bound, split=(), dtype=jnp.bfloat16):
    values = jax.random.normal(stream_key, dims, jnp.float32) * scale
    if len(split) > 0:
        values = levels(stream_key, dims, split, -0.22, 0.18) * values
    return jnp.clip(values, min=-bound, max=bound).astype(dtype)


def gaussian_with(rng, dims, deviation, bound, split, heavy, kind=jnp.bfloat16):
    values = deviation * jax.random.normal(rng, dims, jnp.float32)
    if split:
        values = values * levels(rng, dims, split, -0.22, 0.18)
    return jnp.clip(spiked(values, jax.random.fold_in(rng, 3), *heavy), -bound, bound).astype(kind)


def setup_inputs(seed: int = 0) -> dict:
    key_of = jax.random.split(jax.random.key(seed), 6)
    return {
        "signal": gaussian_with(key_of[0], (CHANNELS, B, B), 1.0, 24.0, ((0, 4), (1, 128)), (1, 2, 128, 5.5)),
        "right_factor": normal_values(key_of[1], (B, B), B ** -0.5, 0.1875, ((0, 4),)),
        "left_factor": normal_values(key_of[2], (B, B), B ** -0.5, 0.1875, ((0, 4),)),
        "gate": normal_values(key_of[3], (CHANNELS, B, B), 1.0, 6.0, ((0, 4), (1, 128))),
        "cotangent": normal_values(key_of[4], (CHANNELS, B, B), 0.1, 1.5, ((0, 4), (1, 128))),
    }


def reference(signal, right_factor, left_factor, gate, cotangent):
    signal_f = signal.astype(jnp.float32)
    right_f = right_factor.astype(jnp.float32)
    left_f = left_factor.astype(jnp.float32)
    inner = jnp.einsum('cij,kj->cik', signal_f, right_f).astype(jnp.bfloat16)
    inner_f = inner.astype(jnp.float32)
    value = jnp.einsum('cik,li->ckl', inner_f, left_f)
    gate_f = gate.astype(jnp.float32)
    cot_f = cotangent.astype(jnp.float32)
    mixed = (gate_f * value).astype(jnp.bfloat16)
    gate_grad = (cot_f * value).astype(jnp.bfloat16)
    value_grad = (gate_f * cot_f).astype(jnp.bfloat16).astype(jnp.float32)
    left_grad = jnp.einsum('ckl,cik->li', value_grad, inner_f)
    inner_grad = jnp.einsum('ckl,li->cik', value_grad, left_f).astype(jnp.bfloat16)
    inner_grad_f = inner_grad.astype(jnp.float32)
    right_grad = jnp.einsum('cik,cij->kj', inner_grad_f, signal_f)
    signal_grad = jnp.einsum('cik,kj->cij', inner_grad_f, right_f).astype(jnp.bfloat16)
    return mixed, right_grad, left_grad, gate_grad, signal_grad
```

```python
import jax
import jax.numpy as jnp
from jax import lax
from jax.sharding import Mesh, PartitionSpec as P

SWAP = [(0, 1), (1, 0)]
SEQ = ("yl", "x", "z")
CHAN = ("yh", "co")


def ordered(own, other, axis, name):
    first = lax.axis_index(name) == 0
    low = jnp.where(first, own, other)
    high = jnp.where(first, other, own)
    return jnp.concatenate([low, high], axis=axis)


def local(signal, right_factor, left_factor, gate, cotangent):
    f32, bf16 = jnp.float32, jnp.bfloat16
    chans, rows, width = signal.shape
    part = right_factor.shape[0]
    group = width // rows
    value_grad = (gate.astype(f32) * cotangent.astype(f32)).astype(bf16)
    packed = jnp.concatenate(
        [
            right_factor,
            left_factor,
            signal.reshape(chans * rows, width),
            value_grad.reshape(chans * rows, width),
        ],
        axis=0,
    )
    far = lax.ppermute(packed, "yh", SWAP)
    pair = jnp.stack([packed, far])
    near = lax.ppermute(pair, "co", SWAP)
    cores = ordered(pair[:, None], near[:, None], 1, "co")
    own_first = lax.axis_index("yh") == 0
    all_rows = jnp.where(own_first, cores, cores[::-1])
    right_full = all_rows[:, :, :part].reshape(4 * part, width)
    left_full = all_rows[:, :, part : 2 * part].reshape(4 * part, width)
    n = chans * rows
    sig = all_rows[:, :, 2 * part : 2 * part + n].reshape(4 * chans, rows, width)
    vgr = all_rows[:, :, 2 * part + n :].reshape(4 * chans, rows, width)
    sig = sig.transpose(1, 0, 2).reshape(4 * n, width)
    vgr = vgr.transpose(1, 0, 2).reshape(4 * n, width)
    inner = jnp.einsum("kj,nj->kn", right_full, sig, preferred_element_type=f32).astype(bf16)
    inner_grad = jnp.einsum("li,nl->in", left_full, vgr, preferred_element_type=f32).astype(bf16)
    both = jnp.concatenate(
        [inner.reshape(group, rows, 4 * n), inner_grad.reshape(group, rows, 4 * n)], axis=1
    )
    turned = lax.all_to_all(both, SEQ, split_axis=0, concat_axis=0, tiled=True)
    swap = lambda t: (
        t.reshape(group, rows, rows, 4 * chans)
        .transpose(0, 2, 1, 3)
        .reshape(width, 4 * n)
    )
    fwd = swap(turned[:, :rows])
    bwd = swap(turned[:, rows:])
    q = lax.axis_index(CHAN)
    vgr_cols = lax.dynamic_slice_in_dim(vgr, q * part, part, axis=1)
    bwd_rows = lax.dynamic_slice_in_dim(bwd, q * part, part, axis=0)
    left_part = jnp.einsum("in,nl->il", fwd, vgr_cols, preferred_element_type=f32).astype(bf16)
    right_part = jnp.einsum("nj,kn->jk", sig, bwd_rows, preferred_element_type=f32).astype(bf16)
    parts = jnp.concatenate(
        [left_part.reshape(group, rows, part), right_part.reshape(group, rows, part)], axis=1
    )
    terms = lax.all_to_all(parts, SEQ, split_axis=0, concat_axis=0, tiled=True)
    grads = jnp.sum(terms.astype(f32), axis=0)
    left_grad = grads[:rows].T
    right_grad = grads[rows:].T
    own = lambda t: lax.dynamic_slice_in_dim(
        t.reshape(width, rows, 4 * chans), q * chans, chans, axis=2
    )
    value = jnp.einsum("ikc,li->ckl", own(fwd), left_full, preferred_element_type=f32)
    mixed = (gate.astype(f32) * value).astype(bf16)
    gate_grad = (cotangent.astype(f32) * value).astype(bf16)
    signal_grad = jnp.einsum(
        "kic,kj->cij", own(bwd), right_full, preferred_element_type=f32
    ).astype(bf16)
    return (mixed, right_grad, left_grad, gate_grad, signal_grad)


def solution(mesh):
    split = Mesh(mesh.devices.reshape(4, 4, 8, 2, 2), SEQ + CHAN)
    rows = P(CHAN, SEQ, None)
    fn = jax.shard_map(
        local,
        mesh=split,
        in_specs=(rows, P(CHAN, None), P(CHAN, None), rows, rows),
        out_specs=(rows, P(CHAN, SEQ), P(CHAN, SEQ), rows, rows),
        check_vma=False,
    )
    return fn
```

```python
import functools

import jax
import jax.numpy as jnp
import numpy as np
from jax import lax
from jax.experimental import pallas as pl
from jax.experimental.pallas import tpu as pltpu
from jax.sharding import Mesh, PartitionSpec as P

SWAP = [(0, 1), (1, 0)]
SEQ = ("yl", "x", "z")
CHAN = ("yh", "co")
F32, BF16 = jnp.float32, jnp.bfloat16
PARAMS = pltpu.CompilerParams(vmem_limit_bytes=48 * 2**20)
VMEM = pl.BlockSpec(memory_space=pltpu.VMEM)
SMEM = pl.BlockSpec(memory_space=pltpu.SMEM)


def dot(a, b, dims=((1,), (0,))):
    return lax.dot_general(a, b, (dims, ((), ())), preferred_element_type=F32)


def first_kernel(n, q_ref, perm_ref, *refs):
    factors, sv, (both_ref, sig_ref, cols_ref), (out, grad) = refs[:4], refs[4:8], refs[8:11], refs[11:]
    part, width = factors[0].shape[0] // 2, factors[0].shape[1]
    rows = both_ref.shape[1] // 2
    q = q_ref[0]
    perm = perm_ref[...]
    sig = dot(perm, jnp.concatenate([s[:n] for s in sv], axis=0)).astype(BF16)
    grad_rows = dot(perm, jnp.concatenate([s[n:] for s in sv], axis=0)).astype(BF16)
    sig_ref[...] = sig
    for a in range(4):
        grad[a] = grad_rows[:, a * part : (a + 1) * part]
    cols_ref[...] = grad[q]
    total = jnp.zeros((4 * n, width), F32)
    for r in range(4):
        a = q ^ r
        inner = dot(factors[r][:part], sig, ((1,), (1,)))
        out[pl.ds(a * (part // rows), part // rows), :rows, :] = inner.reshape(part // rows, rows, 4 * n)
        total += dot(grad[a], factors[r][part:])
    out[:, rows:, :] = total.T.reshape(width // rows, rows, 4 * n)
    both_ref[...] = out[...].astype(BF16)


def second_kernel(q_ref, turned_ref, sig_t_ref, cols_ref, parts_ref, fwd_ref, bwd_ref, held, swapped, out):
    group, both, lanes = turned_ref.shape
    rows = both // 2
    part = cols_ref.shape[1]
    wide = lanes // rows
    held[...] = turned_ref[...].astype(F32).reshape(group * both, lanes)
    block = lax.broadcasted_iota(jnp.int32, (group, lanes), 1) // wide
    for half, ref in ((0, fwd_ref), (1, bwd_ref)):
        pieces = [held[pl.ds(half * rows + k, group, stride=both), :] for k in range(rows)]
        for i in range(rows):
            acc = pieces[i]
            for k in range(rows):
                if k != i:
                    acc = jnp.where(block == k, pltpu.roll(pieces[k], (k - i) % rows * wide, 1), acc)
            swapped[pl.ds(i, group, stride=rows), :] = acc
        ref[...] = swapped[...].astype(BF16)
        if half == 0:
            left = dot(ref[...], cols_ref[...])
            out[:, :rows, :] = left.reshape(group, rows, part)
        else:
            mine = swapped[pl.ds(pl.multiple_of(q_ref[0] * part, part), part), :].T.astype(BF16)
            right = dot(sig_t_ref[...], mine)
            out[:, rows:, :] = right.reshape(group, rows, part)
    parts_ref[...] = out[...].astype(BF16)


def third_kernel(n, q_ref, own_ref, fwd_ref, bwd_ref, gate_ref, cot_ref, *refs):
    factors, (mixed_ref, gate_grad_ref, signal_grad_ref), (value, back) = refs[:4], refs[4:7], refs[7:]
    part, width = factors[0].shape[0] // 2, factors[0].shape[1]
    shape = gate_ref.shape
    q = q_ref[0]
    own = own_ref[...]
    ahead = dot(own, fwd_ref[...], ((1,), (1,))).astype(BF16)
    behind = dot(own, bwd_ref[...], ((1,), (1,))).astype(BF16)
    for a in range(4):
        back[a] = behind[:, a * part : (a + 1) * part]
    grad = jnp.zeros((n, width), F32)
    for r in range(4):
        a = q ^ r
        value[a] = dot(ahead, factors[r][part:], ((1,), (1,)))
        grad += dot(back[a], factors[r][:part])
    whole = jnp.concatenate([value[a] for a in range(4)], axis=1).reshape(shape)
    mixed_ref[...] = (gate_ref[...].astype(F32) * whole).astype(BF16)
    gate_grad_ref[...] = (cot_ref[...].astype(F32) * whole).astype(BF16)
    signal_grad_ref[...] = grad.reshape(shape).astype(BF16)


def local(signal, right_factor, left_factor, gate, cotangent):
    chans, rows, width = signal.shape
    part = right_factor.shape[0]
    group, n = width // rows, chans * rows
    lanes = 4 * n
    struct = jax.ShapeDtypeStruct
    low, count = lax.axis_size("yl"), 2 * lax.axis_size("yl")
    mirror = []
    for y in range(count):
        t = count - 1 - y
        mirror.append(((y % low) * 2 + y // low, (t % low) * 2 + t // low))
    value_grad = (gate.astype(F32) * cotangent.astype(F32)).astype(BF16)
    factors = jnp.concatenate([right_factor, left_factor], axis=0)
    sv = jnp.concatenate([signal.reshape(n, width), value_grad.reshape(n, width)], axis=0)
    far_factors = lax.ppermute(factors, ("yl", "yh"), mirror)
    far_sv = lax.ppermute(sv, "yh", SWAP)
    near_factors = lax.ppermute(factors, "co", SWAP)
    near_sv = lax.ppermute(sv, "co", SWAP)
    cross_factors = lax.ppermute(far_factors, "co", SWAP)
    cross_sv = lax.ppermute(far_sv, "co", SWAP)
    all_factors = (factors, near_factors, far_factors, cross_factors)
    all_sv = (sv, near_sv, far_sv, cross_sv)
    q = lax.axis_index(CHAN).astype(jnp.int32).reshape(1)

    to = np.arange(lanes)
    pos, quarter, chan = to // (4 * chans), to // chans % 4, to % chans
    perm = np.zeros((lanes, lanes), np.float32)
    perm[to, quarter * n + chan * rows + pos] = 1
    mine = np.arange(n)
    own = np.zeros((n, lanes), np.float32)
    own[mine, mine % rows * 4 * chans + mine // rows] = 1

    both, sig, cols = pl.pallas_call(
        functools.partial(first_kernel, n),
        out_shape=(
            struct((group, 2 * rows, lanes), BF16),
            struct((lanes, width), BF16),
            struct((lanes, part), BF16),
        ),
        in_specs=[SMEM] + [VMEM] * 9,
        out_specs=(VMEM,) * 3,
        scratch_shapes=[pltpu.VMEM((group, 2 * rows, lanes), F32), pltpu.VMEM((4, lanes, part), BF16)],
        compiler_params=PARAMS,
        name="first",
    )(q, jnp.asarray(perm, BF16), *all_factors, *all_sv)
    turned = lax.all_to_all(both, SEQ, split_axis=0, concat_axis=0, tiled=True)
    parts, fwd, bwd = pl.pallas_call(
        second_kernel,
        out_shape=(
            struct((group, 2 * rows, part), BF16),
            struct((width, lanes), BF16),
            struct((width, lanes), BF16),
        ),
        in_specs=[SMEM] + [VMEM] * 3,
        out_specs=(VMEM,) * 3,
        scratch_shapes=[
            pltpu.VMEM((group * 2 * rows, lanes), F32),
            pltpu.VMEM((width, lanes), F32),
            pltpu.VMEM((group, 2 * rows, part), F32),
        ],
        compiler_params=PARAMS,
        name="second",
    )(q, turned, sig.T, cols)
    terms = lax.all_to_all(parts, SEQ, split_axis=0, concat_axis=0, tiled=True)
    mixed, gate_grad, signal_grad = pl.pallas_call(
        functools.partial(third_kernel, n),
        out_shape=(struct(signal.shape, BF16),) * 3,
        in_specs=[SMEM] + [VMEM] * 9,
        out_specs=(VMEM,) * 3,
        scratch_shapes=[pltpu.VMEM((4, n, part), F32), pltpu.VMEM((4, n, part), BF16)],
        compiler_params=PARAMS,
        cost_estimate=pl.CostEstimate(flops=10**9, bytes_accessed=6 * 2**20, transcendentals=0),
        name="third",
    )(q, jnp.asarray(own, BF16), fwd, bwd, gate, cotangent, *all_factors)
    grads = jnp.sum(terms.astype(F32), axis=0)
    return (mixed, grads[rows:].T, grads[:rows].T, gate_grad, signal_grad)


def solution(mesh):
    split = Mesh(mesh.devices.reshape(4, 4, 8, 2, 2), SEQ + CHAN)
    rows = P(CHAN, SEQ, None)
    return jax.shard_map(
        local,
        mesh=split,
        in_specs=(rows, P(CHAN, None), P(CHAN, None), rows, rows),
        out_specs=(rows, P(CHAN, SEQ), P(CHAN, SEQ), rows, rows),
        check_vma=False,
    )
```

```python
import functools

import jax
import jax.numpy as jnp
import numpy as np
from jax import lax
from jax.experimental import pallas as pl
from jax.experimental.pallas import tpu as pltpu
from jax.sharding import Mesh, PartitionSpec as P

SWAP = [(0, 1), (1, 0)]
SEQ = ("yl", "x", "z")
CHAN = ("yh", "co")
F32, BF16 = jnp.float32, jnp.bfloat16
PARAMS = pltpu.CompilerParams(vmem_limit_bytes=24 * 2**20)
VMEM = pl.BlockSpec(memory_space=pltpu.VMEM)
SMEM = pl.BlockSpec(memory_space=pltpu.SMEM)


def dot(a, b, dims=((1,), (0,))):
    return lax.dot_general(a, b, (dims, ((), ())), preferred_element_type=F32)


def first_kernel(n, place_ref, perm_ref, own_ref, near_ref, far_ref, cross_ref, *refs):
    far_sv, cross_sv, both_ref, sig_ref, cols_ref, right_ref, left_ref, out, grad = refs
    width = own_ref.shape[1]
    part = width // 4
    pieces = far_ref.shape[0]
    piece = part // pieces
    rows = both_ref.shape[1] // 2
    q = place_ref[0]
    for r, ref in ((0, own_ref), (1, near_ref)):
        at = pl.ds(pl.multiple_of((q ^ r) * part, part), part)
        right_ref[at, :] = ref[:part]
        left_ref[at, :] = ref[part : 2 * part]
    for r, ref in ((2, far_ref), (3, cross_ref)):
        for p in range(pieces):
            at = pl.ds(pl.multiple_of((q ^ r) * part + place_ref[1 + p] * piece, piece), piece)
            right_ref[at, :] = ref[p, :piece]
            left_ref[at, :] = ref[p, piece:]
    perm = perm_ref[...]
    acts = (own_ref[2 * part :], near_ref[2 * part :], far_sv[...], cross_sv[...])
    sig = dot(perm, jnp.concatenate([t[:n] for t in acts], axis=0)).astype(BF16)
    grad_rows = dot(perm, jnp.concatenate([t[n:] for t in acts], axis=0)).astype(BF16)
    sig_ref[...] = sig
    for a in range(4):
        grad[a] = grad_rows[:, a * part : (a + 1) * part]
    cols_ref[...] = grad[q]
    inner = dot(right_ref[...], sig, ((1,), (1,)))
    out[:, :rows, :] = inner.reshape(width // rows, rows, 4 * n)
    total = dot(grad_rows, left_ref[...])
    out[:, rows:, :] = total.T.reshape(width // rows, rows, 4 * n)
    both_ref[...] = out[...].astype(BF16)


def second_kernel(q_ref, turned_ref, sig_t_ref, cols_ref, parts_ref, fwd_ref, bwd_ref, held, swapped, out):
    group, both, lanes = turned_ref.shape
    rows = both // 2
    part = cols_ref.shape[1]
    wide = lanes // rows
    held[...] = turned_ref[...].astype(F32).reshape(group * both, lanes)
    block = lax.broadcasted_iota(jnp.int32, (group, lanes), 1) // wide
    for half, ref in ((0, fwd_ref), (1, bwd_ref)):
        pieces = [held[pl.ds(half * rows + k, group, stride=both), :] for k in range(rows)]
        for i in range(rows):
            acc = pieces[i]
            for k in range(rows):
                if k != i:
                    acc = jnp.where(block == k, pltpu.roll(pieces[k], (k - i) % rows * wide, 1), acc)
            swapped[pl.ds(i, group, stride=rows), :] = acc
        ref[...] = swapped[...].astype(BF16)
        if half == 0:
            left = dot(ref[...], cols_ref[...])
            out[:, :rows, :] = left.reshape(group, rows, part)
        else:
            mine = swapped[pl.ds(pl.multiple_of(q_ref[0] * part, part), part), :].T.astype(BF16)
            right = dot(sig_t_ref[...], mine)
            out[:, rows:, :] = right.reshape(group, rows, part)
    parts_ref[...] = out[...].astype(BF16)


def third_kernel(own_ref, fwd_ref, bwd_ref, gate_ref, cot_ref, right_ref, left_ref, mixed_ref, gate_grad_ref, signal_grad_ref):
    shape = gate_ref.shape
    own = own_ref[...]
    ahead = dot(own, fwd_ref[...], ((1,), (1,))).astype(BF16)
    behind = dot(own, bwd_ref[...], ((1,), (1,))).astype(BF16)
    value = dot(ahead, left_ref[...], ((1,), (1,))).reshape(shape)
    mixed_ref[...] = (gate_ref[...].astype(F32) * value).astype(BF16)
    gate_grad_ref[...] = (cot_ref[...].astype(F32) * value).astype(BF16)
    signal_grad_ref[...] = dot(behind, right_ref[...]).reshape(shape).astype(BF16)


def local(signal, right_factor, left_factor, gate, cotangent):
    chans, rows, width = signal.shape
    part = right_factor.shape[0]
    group, n = width // rows, chans * rows
    lanes = 4 * n
    struct = jax.ShapeDtypeStruct
    low, count = lax.axis_size("yl"), 2 * lax.axis_size("yl")
    mirror = []
    for y in range(count):
        t = count - 1 - y
        mirror.append(((y % low) * 2 + y // low, (t % low) * 2 + t // low))
    across = lax.axis_size("x")
    piece = part // across
    x = lax.axis_index("x")
    value_grad = (gate.astype(F32) * cotangent.astype(F32)).astype(BF16)
    sv = jnp.concatenate([signal.reshape(n, width), value_grad.reshape(n, width)], axis=0)
    mine = jnp.concatenate(
        [lax.dynamic_slice_in_dim(f, x * piece, piece, axis=0) for f in (right_factor, left_factor)], axis=0
    )
    own = jnp.concatenate([right_factor, left_factor, sv], axis=0)
    far_mine = lax.ppermute(mine, ("yl", "yh"), mirror)
    far_sv = lax.ppermute(sv, "yh", SWAP)
    near = lax.ppermute(own, "co", SWAP)
    far_mine, far_sv, near = lax.optimization_barrier((far_mine, far_sv, near))
    moved = [
        lax.ppermute(far_mine, "x", [(i, (i + d) % across) for i in range(across)]) for d in range(1, across)
    ]
    cross_sv = lax.ppermute(far_sv, "co", SWAP)
    far = jnp.stack([far_mine] + moved)
    cross = lax.ppermute(far, "co", SWAP)
    place = jnp.stack([lax.axis_index(CHAN)] + [lax.rem(x + (across - d), across) for d in range(across)]).astype(jnp.int32)
    q = place[:1]

    to = np.arange(lanes)
    pos, quarter, chan = to // (4 * chans), to // chans % 4, to % chans
    perm = np.zeros((lanes, lanes), np.float32)
    perm[to, quarter * n + chan * rows + pos] = 1
    to = np.arange(n)
    pick = np.zeros((n, lanes), np.float32)
    pick[to, to % rows * 4 * chans + to // rows] = 1

    both, sig, cols, right_full, left_full = pl.pallas_call(
        functools.partial(first_kernel, n),
        out_shape=(
            struct((group, 2 * rows, lanes), BF16),
            struct((lanes, width), BF16),
            struct((lanes, part), BF16),
            struct((width, width), BF16),
            struct((width, width), BF16),
        ),
        in_specs=[SMEM] + [VMEM] * 7,
        out_specs=(VMEM,) * 5,
        scratch_shapes=[pltpu.VMEM((group, 2 * rows, lanes), F32), pltpu.VMEM((4, lanes, part), BF16)],
        compiler_params=PARAMS,
        name="first",
    )(place, jnp.asarray(perm, BF16), own, near, far, cross, far_sv, cross_sv)
    turned = lax.all_to_all(both, SEQ, split_axis=0, concat_axis=0, tiled=True)
    parts, fwd, bwd = pl.pallas_call(
        second_kernel,
        out_shape=(
            struct((group, 2 * rows, part), BF16),
            struct((width, lanes), BF16),
            struct((width, lanes), BF16),
        ),
        in_specs=[SMEM] + [VMEM] * 3,
        out_specs=(VMEM,) * 3,
        scratch_shapes=[
            pltpu.VMEM((group * 2 * rows, lanes), F32),
            pltpu.VMEM((width, lanes), F32),
            pltpu.VMEM((group, 2 * rows, part), F32),
        ],
        compiler_params=PARAMS,
        name="second",
    )(q, turned, sig.T, cols)
    terms = lax.all_to_all(parts, SEQ, split_axis=0, concat_axis=0, tiled=True)
    mixed, gate_grad, signal_grad = pl.pallas_call(
        third_kernel,
        out_shape=(struct(signal.shape, BF16),) * 3,
        in_specs=[VMEM] * 7,
        out_specs=(VMEM,) * 3,
        compiler_params=PARAMS,
        cost_estimate=pl.CostEstimate(flops=10**9, bytes_accessed=6 * 2**20, transcendentals=0),
        name="third",
    )(jnp.asarray(pick, BF16), fwd, bwd, gate, cotangent, right_full, left_full)
    grads = jnp.sum(terms.astype(F32), axis=0)
    return (mixed, grads[rows:].T, grads[:rows].T, gate_grad, signal_grad)


def solution(mesh):
    split = Mesh(mesh.devices.reshape(4, 4, 8, 2, 2), SEQ + CHAN)
    rows = P(CHAN, SEQ, None)
    return jax.shard_map(
        local,
        mesh=split,
        in_specs=(rows, P(CHAN, None), P(CHAN, None), rows, rows),
        out_specs=(rows, P(CHAN, SEQ), P(CHAN, SEQ), rows, rows),
        check_vma=False,
    )
```

```python
import functools

import jax
import jax.numpy as jnp
import numpy as np
from jax import lax
from jax.experimental import pallas as pl
from jax.experimental.pallas import tpu as pltpu
from jax.sharding import Mesh, PartitionSpec as P

SWAP = [(0, 1), (1, 0)]
SEQ = ("yl", "x", "z")
CHAN = ("yh", "co")
F32, BF16 = jnp.float32, jnp.bfloat16
PARAMS = pltpu.CompilerParams(vmem_limit_bytes=24 * 2**20)
VMEM = pl.BlockSpec(memory_space=pltpu.VMEM)
SMEM = pl.BlockSpec(memory_space=pltpu.SMEM)


def dot(a, b, dims=((1,), (0,))):
    return lax.dot_general(a, b, (dims, ((), ())), preferred_element_type=F32)


def first_kernel(n, q_ref, perm_ref, own_ref, near_ref, far_ref, cross_ref, *refs):
    far_sv, cross_sv, both_ref, sig_t_ref, cols_ref, right_ref, left_ref, out, grad = refs
    width = own_ref.shape[1]
    part = width // 4
    pieces = far_ref.shape[0]
    piece = part // pieces
    rows = both_ref.shape[1] // 2
    q = q_ref[0]
    for r, ref in ((0, own_ref), (1, near_ref)):
        at = pl.ds(pl.multiple_of((q ^ r) * part, part), part)
        right_ref[at, :] = ref[:part]
        left_ref[at, :] = ref[part : 2 * part]
    for r, ref in ((2, far_ref), (3, cross_ref)):
        for p in range(pieces):
            at = pl.ds(pl.multiple_of((q ^ r) * part + p * piece, piece), piece)
            right_ref[at, :] = ref[p, :piece]
            left_ref[at, :] = ref[p, piece:]
    perm = perm_ref[...]
    acts = (own_ref[2 * part :], near_ref[2 * part :], far_sv[...], cross_sv[...])
    sig = dot(perm, jnp.concatenate([t[:n] for t in acts], axis=0))
    sig_t_ref[...] = sig.T.astype(BF16)
    sig = sig.astype(BF16)
    grad_rows = dot(perm, jnp.concatenate([t[n:] for t in acts], axis=0)).astype(BF16)
    for a in range(4):
        grad[a] = grad_rows[:, a * part : (a + 1) * part]
    cols_ref[...] = grad[q]
    inner = dot(right_ref[...], sig, ((1,), (1,)))
    out[:, :rows, :] = inner.reshape(width // rows, rows, 4 * n)
    total = dot(grad_rows, left_ref[...])
    out[:, rows:, :] = total.T.reshape(width // rows, rows, 4 * n)
    both_ref[...] = out[...].astype(BF16)


def second_kernel(q_ref, turned_ref, sig_t_ref, cols_ref, pick_ref, gate_ref, cot_ref, right_ref, left_ref, *refs):
    parts_ref, mixed_ref, gate_grad_ref, signal_grad_ref, held, swapped, out = refs
    group, both, lanes = turned_ref.shape
    rows = both // 2
    part = cols_ref.shape[1]
    wide = lanes // rows
    shape = gate_ref.shape
    pick = pick_ref[...]
    held[...] = turned_ref[...].astype(F32).reshape(group * both, lanes)
    block = lax.broadcasted_iota(jnp.int32, (group, lanes), 1) // wide
    for half in range(2):
        pieces = [held[pl.ds(half * rows + k, group, stride=both), :] for k in range(rows)]
        for i in range(rows):
            acc = pieces[i]
            for k in range(rows):
                if k != i:
                    acc = jnp.where(block == k, pltpu.roll(pieces[k], (k - i) % rows * wide, 1), acc)
            swapped[pl.ds(i, group, stride=rows), :] = acc
        moved = swapped[...].astype(BF16)
        mine = dot(pick, moved, ((1,), (1,))).astype(BF16)
        if half == 0:
            left = dot(moved, cols_ref[...])
            out[:, :rows, :] = left.reshape(group, rows, part)
            value = dot(mine, left_ref[...], ((1,), (1,))).reshape(shape)
            mixed_ref[...] = (gate_ref[...].astype(F32) * value).astype(BF16)
            gate_grad_ref[...] = (cot_ref[...].astype(F32) * value).astype(BF16)
        else:
            own = swapped[pl.ds(pl.multiple_of(q_ref[0] * part, part), part), :].T.astype(BF16)
            right = dot(sig_t_ref[...], own)
            out[:, rows:, :] = right.reshape(group, rows, part)
            signal_grad_ref[...] = dot(mine, right_ref[...]).reshape(shape).astype(BF16)
    parts_ref[...] = out[...].astype(BF16)


def local(signal, right_factor, left_factor, gate, cotangent):
    chans, rows, width = signal.shape
    part = right_factor.shape[0]
    group, n = width // rows, chans * rows
    lanes = 4 * n
    struct = jax.ShapeDtypeStruct
    low, count = lax.axis_size("yl"), 2 * lax.axis_size("yl")
    mirror = []
    for y in range(count):
        t = count - 1 - y
        mirror.append(((y % low) * 2 + y // low, (t % low) * 2 + t // low))
    across = lax.axis_size("x")
    piece = part // across
    x = lax.axis_index("x")
    value_grad = (gate.astype(F32) * cotangent.astype(F32)).astype(BF16)
    sv = jnp.concatenate([signal.reshape(n, width), value_grad.reshape(n, width)], axis=0)
    mine = jnp.concatenate(
        [lax.dynamic_slice_in_dim(f, x * piece, piece, axis=0) for f in (right_factor, left_factor)], axis=0
    )
    own = jnp.concatenate([right_factor, left_factor, sv], axis=0)
    far_mine = lax.ppermute(mine, ("yl", "yh"), mirror)
    far_sv = lax.ppermute(sv, "yh", SWAP)
    near = lax.ppermute(own, "co", SWAP)
    far_mine, far_sv, near = lax.optimization_barrier((far_mine, far_sv, near))
    cross_sv = lax.ppermute(far_sv, "co", SWAP)
    copies = jnp.broadcast_to(far_mine[None], (across,) + far_mine.shape)
    far = lax.all_to_all(copies, "x", split_axis=0, concat_axis=0, tiled=True)
    cross = lax.ppermute(far, "co", SWAP)
    q = lax.axis_index(CHAN).astype(jnp.int32).reshape(1)

    to = np.arange(lanes)
    pos, quarter, chan = to // (4 * chans), to // chans % 4, to % chans
    perm = np.zeros((lanes, lanes), np.float32)
    perm[to, quarter * n + chan * rows + pos] = 1
    to = np.arange(n)
    pick = np.zeros((n, lanes), np.float32)
    pick[to, to % rows * 4 * chans + to // rows] = 1

    both, sig_t, cols, right_full, left_full = pl.pallas_call(
        functools.partial(first_kernel, n),
        out_shape=(
            struct((group, 2 * rows, lanes), BF16),
            struct((width, lanes), BF16),
            struct((lanes, part), BF16),
            struct((width, width), BF16),
            struct((width, width), BF16),
        ),
        in_specs=[SMEM] + [VMEM] * 7,
        out_specs=(VMEM,) * 5,
        scratch_shapes=[pltpu.VMEM((group, 2 * rows, lanes), F32), pltpu.VMEM((4, lanes, part), BF16)],
        compiler_params=PARAMS,
        name="first",
    )(q, jnp.asarray(perm, BF16), own, near, far, cross, far_sv, cross_sv)
    turned = lax.all_to_all(both, SEQ, split_axis=0, concat_axis=0, tiled=True)
    parts, mixed, gate_grad, signal_grad = pl.pallas_call(
        second_kernel,
        out_shape=(struct((group, 2 * rows, part), BF16),) + (struct(signal.shape, BF16),) * 3,
        in_specs=[SMEM] + [VMEM] * 8,
        out_specs=(VMEM,) * 4,
        scratch_shapes=[
            pltpu.VMEM((group * 2 * rows, lanes), F32),
            pltpu.VMEM((width, lanes), F32),
            pltpu.VMEM((group, 2 * rows, part), F32),
        ],
        compiler_params=PARAMS,
        name="second",
    )(q, turned, sig_t, cols, jnp.asarray(pick, BF16), gate, cotangent, right_full, left_full)
    terms = lax.all_to_all(parts, SEQ, split_axis=0, concat_axis=0, tiled=True)
    grads = jnp.sum(terms.astype(F32), axis=0)
    return (mixed, grads[rows:].T, grads[:rows].T, gate_grad, signal_grad)


def solution(mesh):
    split = Mesh(mesh.devices.reshape(4, 4, 8, 2, 2), SEQ + CHAN)
    rows = P(CHAN, SEQ, None)
    return jax.shard_map(
        local,
        mesh=split,
        in_specs=(rows, P(CHAN, None), P(CHAN, None), rows, rows),
        out_specs=(rows, P(CHAN, SEQ), P(CHAN, SEQ), rows, rows),
        check_vma=False,
    )
```

```python
import functools

import jax
import jax.numpy as jnp
import numpy as np
from jax import lax
from jax.experimental import pallas as pl
from jax.experimental.pallas import tpu as pltpu
from jax.sharding import Mesh, PartitionSpec as P

SWAP = [(0, 1), (1, 0)]
SEQ = ("yl", "x", "zh", "zl")
SPREAD = ("x", "zl")
CHAN = ("yh", "co")
F32, BF16 = jnp.float32, jnp.bfloat16
PARAMS = pltpu.CompilerParams(vmem_limit_bytes=24 * 2**20)
VMEM = pl.BlockSpec(memory_space=pltpu.VMEM)
SMEM = pl.BlockSpec(memory_space=pltpu.SMEM)


def dot(a, b, dims=((1,), (0,))):
    return lax.dot_general(a, b, (dims, ((), ())), preferred_element_type=F32)


def first_kernel(n, q_ref, perm_ref, own_ref, near_ref, far_ref, cross_ref, *refs):
    both_ref, sig_t_ref, cols_ref, right_ref, left_ref, out, grad = refs
    width = own_ref.shape[1]
    part = width // 4
    pieces = far_ref.shape[0]
    piece = part // pieces
    rows = both_ref.shape[1] // 2
    q = q_ref[0]
    for r, ref in ((0, own_ref), (1, near_ref)):
        at = pl.ds(pl.multiple_of((q ^ r) * part, part), part)
        right_ref[at, :] = ref[:part]
        left_ref[at, :] = ref[part : 2 * part]
    for r, ref in ((2, far_ref), (3, cross_ref)):
        for p in range(pieces):
            at = pl.ds(pl.multiple_of((q ^ r) * part + p * piece, piece), piece)
            right_ref[at, :] = ref[p, :piece]
            left_ref[at, :] = ref[p, piece:]
    perm = perm_ref[...]
    acts = [ref[2 * part + f * 2 * n : 2 * part + (f + 1) * 2 * n] for f in range(2) for ref in (own_ref, near_ref)]
    sig = dot(perm, jnp.concatenate([t[:n] for t in acts], axis=0))
    sig_t_ref[...] = sig.T.astype(BF16)
    sig = sig.astype(BF16)
    grad_rows = dot(perm, jnp.concatenate([t[n:] for t in acts], axis=0)).astype(BF16)
    for a in range(4):
        grad[a] = grad_rows[:, a * part : (a + 1) * part]
    cols_ref[...] = grad[q]
    inner = dot(right_ref[...], sig, ((1,), (1,)))
    out[:, :rows, :] = inner.reshape(width // rows, rows, 4 * n)
    total = dot(grad_rows, left_ref[...])
    out[:, rows:, :] = total.T.reshape(width // rows, rows, 4 * n)
    both_ref[...] = out[...].astype(BF16)


def second_kernel(q_ref, turned_ref, sig_t_ref, cols_ref, pick_ref, gate_ref, cot_ref, right_ref, left_ref, *refs):
    parts_ref, mixed_ref, gate_grad_ref, signal_grad_ref, held, swapped, out = refs
    group, both, lanes = turned_ref.shape
    rows = both // 2
    part = cols_ref.shape[1]
    wide = lanes // rows
    shape = gate_ref.shape
    pick = pick_ref[...]
    held[...] = turned_ref[...].astype(F32).reshape(group * both, lanes)
    block = lax.broadcasted_iota(jnp.int32, (group, lanes), 1) // wide
    for half in range(2):
        pieces = [held[pl.ds(half * rows + k, group, stride=both), :] for k in range(rows)]
        for i in range(rows):
            acc = pieces[i]
            for k in range(rows):
                if k != i:
                    acc = jnp.where(block == k, pltpu.roll(pieces[k], (k - i) % rows * wide, 1), acc)
            swapped[pl.ds(i, group, stride=rows), :] = acc
        moved = swapped[...].astype(BF16)
        mine = dot(pick, moved, ((1,), (1,))).astype(BF16)
        if half == 0:
            left = dot(moved, cols_ref[...])
            out[:, :rows, :] = left.reshape(group, rows, part)
            value = dot(mine, left_ref[...], ((1,), (1,))).reshape(shape)
            mixed_ref[...] = (gate_ref[...].astype(F32) * value).astype(BF16)
            gate_grad_ref[...] = (cot_ref[...].astype(F32) * value).astype(BF16)
        else:
            own = swapped[pl.ds(pl.multiple_of(q_ref[0] * part, part), part), :].T.astype(BF16)
            right = dot(sig_t_ref[...], own)
            out[:, rows:, :] = right.reshape(group, rows, part)
            signal_grad_ref[...] = dot(mine, right_ref[...]).reshape(shape).astype(BF16)
    parts_ref[...] = out[...].astype(BF16)


def local(signal, right_factor, left_factor, gate, cotangent):
    chans, rows, width = signal.shape
    part = right_factor.shape[0]
    group, n = width // rows, chans * rows
    lanes = 4 * n
    struct = jax.ShapeDtypeStruct
    low, count = lax.axis_size("yl"), 2 * lax.axis_size("yl")
    mirror = []
    for y in range(count):
        t = count - 1 - y
        mirror.append(((y % low) * 2 + y // low, (t % low) * 2 + t // low))
    across = lax.axis_size(SPREAD)
    piece = part // across
    start = lax.axis_index(SPREAD) * piece
    value_grad = (gate.astype(F32) * cotangent.astype(F32)).astype(BF16)
    sv = jnp.concatenate([signal.reshape(n, width), value_grad.reshape(n, width)], axis=0)
    mine = jnp.concatenate(
        [lax.dynamic_slice_in_dim(f, start, piece, axis=0) for f in (right_factor, left_factor)], axis=0
    )
    far_mine = lax.ppermute(mine, ("yl", "yh"), mirror)
    far_sv = lax.ppermute(sv, "yh", SWAP)
    far_mine, far_sv = lax.optimization_barrier((far_mine, far_sv))
    own = jnp.concatenate([right_factor, left_factor, sv, far_sv], axis=0)
    near = lax.ppermute(own, "co", SWAP)
    copies = jnp.broadcast_to(far_mine[None], (across,) + far_mine.shape)
    far = lax.all_to_all(copies, SPREAD, split_axis=0, concat_axis=0, tiled=True)
    cross = lax.ppermute(far, "co", SWAP)
    q = lax.axis_index(CHAN).astype(jnp.int32).reshape(1)

    to = np.arange(lanes)
    pos, quarter, chan = to // (4 * chans), to // chans % 4, to % chans
    perm = np.zeros((lanes, lanes), np.float32)
    perm[to, quarter * n + chan * rows + pos] = 1
    to = np.arange(n)
    pick = np.zeros((n, lanes), np.float32)
    pick[to, to % rows * 4 * chans + to // rows] = 1

    both, sig_t, cols, right_full, left_full = pl.pallas_call(
        functools.partial(first_kernel, n),
        out_shape=(
            struct((group, 2 * rows, lanes), BF16),
            struct((width, lanes), BF16),
            struct((lanes, part), BF16),
            struct((width, width), BF16),
            struct((width, width), BF16),
        ),
        in_specs=[SMEM] + [VMEM] * 5,
        out_specs=(VMEM,) * 5,
        scratch_shapes=[pltpu.VMEM((group, 2 * rows, lanes), F32), pltpu.VMEM((4, lanes, part), BF16)],
        compiler_params=PARAMS,
        name="first",
    )(q, jnp.asarray(perm, BF16), own, near, far, cross)
    turned = lax.all_to_all(both, SEQ, split_axis=0, concat_axis=0, tiled=True)
    parts, mixed, gate_grad, signal_grad = pl.pallas_call(
        second_kernel,
        out_shape=(struct((group, 2 * rows, part), BF16),) + (struct(signal.shape, BF16),) * 3,
        in_specs=[SMEM] + [VMEM] * 8,
        out_specs=(VMEM,) * 4,
        scratch_shapes=[
            pltpu.VMEM((group * 2 * rows, lanes), F32),
            pltpu.VMEM((width, lanes), F32),
            pltpu.VMEM((group, 2 * rows, part), F32),
        ],
        compiler_params=PARAMS,
        name="second",
    )(q, turned, sig_t, cols, jnp.asarray(pick, BF16), gate, cotangent, right_full, left_full)
    terms = lax.all_to_all(parts, SEQ, split_axis=0, concat_axis=0, tiled=True)
    grads = jnp.sum(terms.astype(F32), axis=0)
    return (mixed, grads[rows:].T, grads[:rows].T, gate_grad, signal_grad)


def solution(mesh):
    split = Mesh(mesh.devices.reshape(4, 4, 4, 2, 2, 2), SEQ + CHAN)
    rows = P(CHAN, SEQ, None)
    return jax.shard_map(
        local,
        mesh=split,
        in_specs=(rows, P(CHAN, None), P(CHAN, None), rows, rows),
        out_specs=(rows, P(CHAN, SEQ), P(CHAN, SEQ), rows, rows),
        check_vma=False,
    )
```

```python
import functools

import jax
import jax.numpy as jnp
import numpy as np
from jax import lax
from jax.experimental import pallas as pl
from jax.experimental.pallas import tpu as pltpu
from jax.sharding import Mesh, PartitionSpec as P

SWAP = [(0, 1), (1, 0)]
SEQ = ("h", "b", "x", "zh", "zl")
TURN = ("h", "x", "zh", "zl")
SPREAD = ("x", "zl")
CHAN = ("yh", "co")
F32, BF16 = jnp.float32, jnp.bfloat16
PARAMS = pltpu.CompilerParams(vmem_limit_bytes=24 * 2**20)
VMEM = pl.BlockSpec(memory_space=pltpu.VMEM)
SMEM = pl.BlockSpec(memory_space=pltpu.SMEM)


def dot(a, b, dims=((1,), (0,))):
    return lax.dot_general(a, b, (dims, ((), ())), preferred_element_type=F32)


def assemble(q, own, near_ref, far_ref, cross_ref, right_ref, left_ref):
    part = right_ref.shape[0] // 4
    pieces, piece = far_ref.shape[0], far_ref.shape[1] // 2
    for r, (right, left) in enumerate((own, (near_ref[:part], near_ref[part : 2 * part]))):
        at = pl.ds(pl.multiple_of((q ^ r) * part, part), part)
        right_ref[at, :] = right
        left_ref[at, :] = left
    for r, ref in ((2, far_ref), (3, cross_ref)):
        for p in range(pieces):
            at = pl.ds(pl.multiple_of((q ^ r) * part + p * piece, piece), piece)
            right_ref[at, :] = ref[p, :piece]
            left_ref[at, :] = ref[p, piece:]


def first_kernel(n, at_ref, perm_ref, own_ref, near_ref, far_ref, cross_ref, acts_ref, pal_ref, *refs):
    both_ref, sig_t_ref, cols_ref, out, held, used, right_ref, left_ref = refs
    q, b, co = at_ref[0], at_ref[1], at_ref[2]
    width = own_ref.shape[1]
    part = width // 4
    rows = both_ref.shape[1] // 4
    own = own_ref[:part], own_ref[part : 2 * part]
    assemble(q, own, near_ref, far_ref, cross_ref, right_ref, left_ref)
    perm = perm_ref[...]
    for other, ref in ((0, acts_ref), (1, pal_ref)):
        slot = b ^ other
        sig = dot(perm, jnp.concatenate([ref[2 * r * n : (2 * r + 1) * n] for r in (0, 2, 1, 3)], axis=0))
        grad = dot(perm, jnp.concatenate([ref[(2 * r + 1) * n : (2 * r + 2) * n] for r in (0, 2, 1, 3)], axis=0))
        for a in range(4):
            held[a] = sig[:, a * part : (a + 1) * part]
        sig_t_ref[slot, :part, :] = held[b].T.astype(BF16)
        sig_t_ref[slot, part:, :] = held[2 + b].T.astype(BF16)
        for a in range(4):
            held[a] = grad[:, a * part : (a + 1) * part]
        cols_ref[slot] = held[q].astype(BF16)
        used[slot] = grad.astype(BF16)
        if other == 0:
            inner = dot(right_ref[...], sig.astype(BF16), ((1,), (1,)))
    turned = dot(used[co], left_ref[...]).T
    group = part // rows
    for h in range(2):
        for c in range(2):
            at = (2 * h + c) * part
            block = inner[at : at + part].reshape(group, rows, 4 * n)
            out[h * group : (h + 1) * group, c * rows : (c + 1) * rows, :] = block
            block = turned[at : at + part].reshape(group, rows, 4 * n)
            out[h * group : (h + 1) * group, (2 + c) * rows : (3 + c) * rows, :] = block
    both_ref[...] = out[...].astype(BF16)


def second_kernel(at_ref, turned_ref, sig_t_ref, cols_ref, pick_ref, *refs):
    parts_ref, ahead_ref, ahead_out_ref, behind_ref, behind_out_ref, held, swapped, out, picked = refs
    b, yh = at_ref[1], at_ref[3]
    group, count, lanes = turned_ref.shape
    rows = count // 4
    part = cols_ref.shape[2]
    wide = lanes // rows
    held[...] = turned_ref[...].astype(F32).reshape(group * count, lanes)
    block = lax.broadcasted_iota(jnp.int32, (group, lanes), 1) // wide
    for half in range(2):
        for c in range(2):
            first = (2 * half + c) * rows
            pieces = [held[pl.ds(first + k, group, stride=count), :] for k in range(rows)]
            for i in range(rows):
                acc = pieces[i]
                for k in range(rows):
                    if k != i:
                        acc = jnp.where(block == k, pltpu.roll(pieces[k], (k - i) % rows * wide, 1), acc)
                swapped[c, pl.ds(i, group, stride=rows), :] = acc
        if half == 0:
            total = 0.0
            for c in range(2):
                moved = swapped[c].astype(BF16)
                total += dot(moved, cols_ref[c])
                picked[c] = dot(pick_ref[0], moved, ((1,), (1,)))
            out[:, :rows, :] = total.reshape(group, rows, part)
            ahead_ref[...] = picked[b].astype(BF16)
            ahead_out_ref[...] = picked[1 - b].astype(BF16)
        else:
            total = 0.0
            for c in range(2):
                mine = swapped[c, pl.ds(pl.multiple_of(yh * part, part), part), :].T.astype(BF16)
                total += dot(sig_t_ref[c], mine)
            out[:, rows:, :] = total.reshape(group, rows, part)
            moved = swapped[b].astype(BF16)
            behind_ref[...] = dot(pick_ref[0], moved, ((1,), (1,))).astype(BF16)
            behind_out_ref[...] = dot(pick_ref[1], moved, ((1,), (1,))).astype(BF16)
    parts_ref[...] = out[...].astype(BF16)


def third_kernel(at_ref, ahead_ref, ahead_in_ref, behind_ref, behind_in_ref, gate_ref, cot_ref, *refs):
    factors, (mixed_ref, gate_grad_ref, signal_grad_ref, ahead, behind, right_ref, left_ref) = refs[:5], refs[5:]
    b, co = at_ref[1], at_ref[2]
    assemble(at_ref[0], (factors[0][...], factors[1][...]), *factors[2:], right_ref, left_ref)
    shape = gate_ref.shape
    part = ahead.shape[2]
    for h in range(2):
        at = slice(h * part, (h + 1) * part)
        ahead[2 * h + b] = ahead_ref[:, at]
        ahead[2 * h + 1 - b] = ahead_in_ref[:, at]
        behind[2 * h + co] = behind_ref[:, at]
        behind[2 * h + 1 - co] = behind_in_ref[:, at]
    every = jnp.concatenate([ahead[a] for a in range(4)], axis=1)
    value = dot(every, left_ref[...], ((1,), (1,))).reshape(shape)
    mixed_ref[...] = (gate_ref[...].astype(F32) * value).astype(BF16)
    gate_grad_ref[...] = (cot_ref[...].astype(F32) * value).astype(BF16)
    every = jnp.concatenate([behind[a] for a in range(4)], axis=1)
    signal_grad_ref[...] = dot(every, right_ref[...]).reshape(shape).astype(BF16)


def local(signal, right_factor, left_factor, gate, cotangent):
    chans, rows, width = signal.shape
    part = right_factor.shape[0]
    group, n = width // rows, chans * rows
    lanes = 4 * n
    struct = jax.ShapeDtypeStruct
    low = lax.axis_size(("h", "b"))
    count = 2 * low
    mirror = []
    for y in range(count):
        t = count - 1 - y
        mirror.append(((y % low) * 2 + y // low, (t % low) * 2 + t // low))
    across = lax.axis_size(SPREAD)
    piece = part // across
    start = lax.axis_index(SPREAD) * piece
    value_grad = (gate.astype(F32) * cotangent.astype(F32)).astype(BF16)
    sv = jnp.concatenate([signal.reshape(n, width), value_grad.reshape(n, width)], axis=0)
    mine = jnp.concatenate(
        [lax.dynamic_slice_in_dim(f, start, piece, axis=0) for f in (right_factor, left_factor)], axis=0
    )
    far_mine = lax.ppermute(mine, ("h", "b", "yh"), mirror)
    far_sv = lax.ppermute(sv, "yh", SWAP)
    far_mine, far_sv = lax.optimization_barrier((far_mine, far_sv))
    own = jnp.concatenate([right_factor, left_factor, sv, far_sv], axis=0)
    near = lax.ppermute(own, "co", SWAP)
    copies = jnp.broadcast_to(far_mine[None], (across,) + far_mine.shape)
    far = lax.all_to_all(copies, SPREAD, split_axis=0, concat_axis=0, tiled=True)
    acts = jnp.concatenate([own[2 * part :], near[2 * part :]], axis=0)
    pal = lax.ppermute(acts, "b", SWAP)
    far, pal = lax.optimization_barrier((far, pal))
    cross = lax.ppermute(far, "co", SWAP)
    at = jnp.stack([lax.axis_index(a) for a in (CHAN, "b", "co", "yh")]).astype(jnp.int32)

    to = np.arange(lanes)
    pos, quarter, chan = to // (4 * chans), to // chans % 4, to % chans
    perm = np.zeros((lanes, lanes), np.float32)
    perm[to, quarter * n + chan * rows + pos] = 1
    to = np.arange(n)
    pick = np.zeros((2, n, lanes), np.float32)
    for r in range(2):
        pick[r, to, to % rows * 4 * chans + r * chans + to // rows] = 1

    half, both_halves = group // 2, 2 * part
    both, sig_t, cols = pl.pallas_call(
        functools.partial(first_kernel, n),
        out_shape=(
            struct((half, 4 * rows, lanes), BF16),
            struct((2, both_halves, lanes), BF16),
            struct((2, lanes, part), BF16),
        ),
        in_specs=[SMEM] + [VMEM] * 7,
        out_specs=(VMEM,) * 3,
        scratch_shapes=[
            pltpu.VMEM((half, 4 * rows, lanes), F32),
            pltpu.VMEM((4, lanes, part), F32),
            pltpu.VMEM((2, lanes, width), BF16),
            pltpu.VMEM((width, width), BF16),
            pltpu.VMEM((width, width), BF16),
        ],
        compiler_params=PARAMS,
        name="first",
    )(at, jnp.asarray(perm, BF16), own, near, far, cross, acts, pal)
    turned = lax.all_to_all(both, TURN, split_axis=0, concat_axis=0, tiled=True)
    parts, ahead, ahead_out, behind, behind_out = pl.pallas_call(
        second_kernel,
        out_shape=(struct((half, 2 * rows, part), BF16),) + (struct((n, both_halves), BF16),) * 4,
        in_specs=[SMEM] + [VMEM] * 4,
        out_specs=(VMEM,) * 5,
        scratch_shapes=[
            pltpu.VMEM((half * 4 * rows, lanes), F32),
            pltpu.VMEM((2, both_halves, lanes), F32),
            pltpu.VMEM((half, 2 * rows, part), F32),
            pltpu.VMEM((2, n, both_halves), F32),
        ],
        compiler_params=PARAMS,
        name="second",
    )(at, turned, sig_t, cols, jnp.asarray(pick, BF16))
    ahead_in = lax.ppermute(ahead_out, "b", SWAP)
    behind_in = lax.ppermute(behind_out, "co", SWAP)
    terms = lax.all_to_all(parts, TURN, split_axis=0, concat_axis=0, tiled=True)
    mixed, gate_grad, signal_grad = pl.pallas_call(
        third_kernel,
        out_shape=(struct(signal.shape, BF16),) * 3,
        in_specs=[SMEM] + [VMEM] * 11,
        out_specs=(VMEM,) * 3,
        scratch_shapes=[pltpu.VMEM((4, n, part), BF16)] * 2 + [pltpu.VMEM((width, width), BF16)] * 2,
        compiler_params=PARAMS,
        cost_estimate=pl.CostEstimate(flops=10**9, bytes_accessed=6 * 2**20, transcendentals=0),
        name="third",
    )(at, ahead, ahead_in, behind, behind_in, gate, cotangent, right_factor, left_factor, near, far, cross)
    grads = jnp.sum(terms.astype(F32), axis=0)
    return (mixed, grads[rows:].T, grads[:rows].T, gate_grad, signal_grad)


def solution(mesh):
    split = Mesh(mesh.devices.reshape(2, 2, 4, 4, 2, 2, 2), SEQ + CHAN)
    rows = P(CHAN, SEQ, None)
    return jax.shard_map(
        local,
        mesh=split,
        in_specs=(rows, P(CHAN, None), P(CHAN, None), rows, rows),
        out_specs=(rows, P(CHAN, SEQ), P(CHAN, SEQ), rows, rows),
        check_vma=False,
    )
```

```python
import functools

import jax
import jax.numpy as jnp
from jax import lax
from jax.experimental import pallas as pl
from jax.experimental.pallas import tpu as pltpu
from jax.sharding import Mesh, PartitionSpec as P

SWAP = [(0, 1), (1, 0)]
SEQ = ("h", "b", "x", "zh", "zl")
TURN = ("h", "x", "zh", "zl")
SPREAD = ("x", "zl")
CHAN = ("yh", "co")
F32, BF16 = jnp.float32, jnp.bfloat16
PARAMS = pltpu.CompilerParams(vmem_limit_bytes=24 * 2**20)
VMEM = pl.BlockSpec(memory_space=pltpu.VMEM)
SMEM = pl.BlockSpec(memory_space=pltpu.SMEM)
ANY = pl.BlockSpec(memory_space=pl.ANY)


def dot(a, b, dims=((1,), (0,))):
    return lax.dot_general(a, b, (dims, ((), ())), preferred_element_type=F32)


def assemble(q, blocks, right_ref, left_ref, sems):
    count = right_ref.shape[0] // 4
    piece = right_ref.shape[1]
    own_right, own_left, near_right, near_left, far, cross = blocks
    sources = (
        (own_right, own_left),
        (near_right, near_left),
        (far.at[:, :piece], far.at[:, piece:]),
        (cross.at[:, :piece], cross.at[:, piece:]),
    )
    copies = []
    for r, pair in enumerate(sources):
        for f, (source, target) in enumerate(zip(pair, (right_ref, left_ref))):
            to = target.at[pl.ds((q ^ r) * count, count)]
            copies.append(pltpu.make_async_copy(source, to, sems.at[2 * r + f]))
    for copy in copies:
        copy.start()
    return copies


def one_hot(rows, columns, target):
    row = lax.broadcasted_iota(jnp.int32, (rows, columns), 0)
    column = lax.broadcasted_iota(jnp.int32, (rows, columns), 1)
    return jnp.where(column == target(row), 1.0, 0.0).astype(BF16)


def first_kernel(n, at_ref, *refs):
    blocks, (acts_ref, pal_ref, both_ref, sig_t_ref, cols_ref, out, held, used, right_ref, left_ref, sems) = refs[:6], refs[6:]
    q, b, co = at_ref[0], at_ref[1], at_ref[2]
    copies = assemble(q, blocks, right_ref, left_ref, sems)
    width = acts_ref.shape[1]
    part = width // 4
    rows = both_ref.shape[1] // 4
    chans = n // rows
    perm = one_hot(
        4 * n, 4 * n, lambda o: o // chans % 4 * n + o % chans * rows + o // (4 * chans)
    )
    for other, ref in ((0, acts_ref), (1, pal_ref)):
        slot = b ^ other
        sig = dot(perm, jnp.concatenate([ref[2 * r * n : (2 * r + 1) * n] for r in (0, 2, 1, 3)], axis=0))
        grad = dot(perm, jnp.concatenate([ref[(2 * r + 1) * n : (2 * r + 2) * n] for r in (0, 2, 1, 3)], axis=0))
        for a in range(4):
            held[a] = sig[:, a * part : (a + 1) * part]
        sig_t_ref[slot, :part, :] = held[b].T.astype(BF16)
        sig_t_ref[slot, part:, :] = held[2 + b].T.astype(BF16)
        for a in range(4):
            held[a] = grad[:, a * part : (a + 1) * part]
        cols_ref[slot] = held[q].astype(BF16)
        used[slot] = grad.astype(BF16)
        if other == 0:
            here = sig.astype(BF16)
    for copy in copies:
        copy.wait()
    inner = dot(right_ref[...].reshape(width, width), here, ((1,), (1,)))
    turned = dot(used[co], left_ref[...].reshape(width, width)).T
    group = part // rows
    for h in range(2):
        for c in range(2):
            at = (2 * h + c) * part
            block = inner[at : at + part].reshape(group, rows, 4 * n)
            out[h * group : (h + 1) * group, c * rows : (c + 1) * rows, :] = block
            block = turned[at : at + part].reshape(group, rows, 4 * n)
            out[h * group : (h + 1) * group, (2 + c) * rows : (3 + c) * rows, :] = block
    both_ref[...] = out[...].astype(BF16)


def second_kernel(n, at_ref, turned_ref, sig_t_ref, cols_ref, *refs):
    parts_ref, kept_ref, ahead_out_ref, behind_out_ref, held, swapped, out, picked = refs
    b, yh = at_ref[1], at_ref[3]
    group, count, lanes = turned_ref.shape
    rows = count // 4
    part = cols_ref.shape[2]
    wide = lanes // rows
    chans = n // rows
    pick = [one_hot(n, lanes, lambda m: m % rows * 4 * chans + r * chans + m // rows) for r in range(2)]
    held[...] = turned_ref[...].astype(F32).reshape(group * count, lanes)
    block = lax.broadcasted_iota(jnp.int32, (group, lanes), 1) // wide
    for half in range(2):
        for c in range(2):
            first = (2 * half + c) * rows
            pieces = [held[pl.ds(first + k, group, stride=count), :] for k in range(rows)]
            for i in range(rows):
                acc = pieces[i]
                for k in range(rows):
                    if k != i:
                        acc = jnp.where(block == k, pltpu.roll(pieces[k], (k - i) % rows * wide, 1), acc)
                swapped[c, pl.ds(i, group, stride=rows), :] = acc
        if half == 0:
            total = 0.0
            for c in range(2):
                moved = swapped[c].astype(BF16)
                total += dot(moved, cols_ref[c])
                picked[c] = dot(pick[0], moved, ((1,), (1,)))
            out[:, :rows, :] = total.reshape(group, rows, part)
            kept_ref[0] = picked[b].astype(BF16)
            ahead_out_ref[...] = picked[1 - b].astype(BF16)
        else:
            total = 0.0
            for c in range(2):
                mine = swapped[c, pl.ds(pl.multiple_of(yh * part, part), part), :].T.astype(BF16)
                total += dot(sig_t_ref[c], mine)
            out[:, rows:, :] = total.reshape(group, rows, part)
            moved = swapped[b].astype(BF16)
            kept_ref[1] = dot(pick[0], moved, ((1,), (1,))).astype(BF16)
            behind_out_ref[...] = dot(pick[1], moved, ((1,), (1,))).astype(BF16)
    parts_ref[...] = out[...].astype(BF16)


def third_kernel(at_ref, kept_ref, ahead_in_ref, behind_in_ref, gate_ref, cot_ref, *refs):
    blocks, refs = refs[:6], refs[6:]
    mixed_ref, gate_grad_ref, signal_grad_ref, ahead, behind, right_ref, left_ref, sems = refs
    b, co = at_ref[1], at_ref[2]
    copies = assemble(at_ref[0], blocks, right_ref, left_ref, sems)
    shape = gate_ref.shape
    part = ahead.shape[2]
    for h in range(2):
        at = slice(h * part, (h + 1) * part)
        ahead[2 * h + b] = kept_ref[0, :, at]
        ahead[2 * h + 1 - b] = ahead_in_ref[:, at]
        behind[2 * h + co] = kept_ref[1, :, at]
        behind[2 * h + 1 - co] = behind_in_ref[:, at]
    width = shape[2]
    for copy in copies:
        copy.wait()
    every = jnp.concatenate([ahead[a] for a in range(4)], axis=1)
    value = dot(every, left_ref[...].reshape(width, width), ((1,), (1,))).reshape(shape)
    mixed_ref[...] = (gate_ref[...].astype(F32) * value).astype(BF16)
    gate_grad_ref[...] = (cot_ref[...].astype(F32) * value).astype(BF16)
    every = jnp.concatenate([behind[a] for a in range(4)], axis=1)
    signal_grad_ref[...] = dot(every, right_ref[...].reshape(width, width)).reshape(shape).astype(BF16)


def local(signal, right_factor, left_factor, gate, cotangent):
    chans, rows, width = signal.shape
    part = right_factor.shape[0]
    group, n = width // rows, chans * rows
    lanes = 4 * n
    struct = jax.ShapeDtypeStruct
    low = lax.axis_size(("h", "b"))
    count = 2 * low
    mirror = []
    for y in range(count):
        t = count - 1 - y
        mirror.append(((y % low) * 2 + y // low, (t % low) * 2 + t // low))
    across = lax.axis_size(SPREAD)
    piece = part // across
    start = lax.axis_index(SPREAD) * piece
    value_grad = (gate.astype(F32) * cotangent.astype(F32)).astype(BF16)
    sv = jnp.concatenate([signal.reshape(n, width), value_grad.reshape(n, width)], axis=0)
    mine = jnp.concatenate(
        [lax.dynamic_slice_in_dim(f, start, piece, axis=0) for f in (right_factor, left_factor)], axis=0
    )
    far_mine = lax.ppermute(mine, ("h", "b", "yh"), mirror)
    far_sv = lax.ppermute(sv, "yh", SWAP)
    far_mine, far_sv, sv, right, left = lax.optimization_barrier((far_mine, far_sv, sv, right_factor, left_factor))
    copies = jnp.broadcast_to(far_mine[None], (across,) + far_mine.shape)
    far = lax.all_to_all(copies, SPREAD, split_axis=0, concat_axis=0, tiled=True)
    half_acts = jnp.concatenate([sv, far_sv], axis=0)
    acts = jnp.concatenate([half_acts, lax.ppermute(half_acts, "co", SWAP)], axis=0)
    pal = lax.ppermute(acts, "b", SWAP)
    near_right, near_left = (lax.ppermute(f, "co", SWAP) for f in (right, left))
    far, pal, near_right, near_left = lax.optimization_barrier((far, pal, near_right, near_left))
    cross = lax.ppermute(far, "co", SWAP)
    in_hbm = functools.partial(pltpu.with_memory_space_constraint, memory_space=pltpu.HBM)
    near = [f.reshape(across, piece, width) for f in (right_factor, left_factor, near_right, near_left)]
    blocks = [in_hbm(f) for f in (*near, far)]
    at = jnp.stack([lax.axis_index(a) for a in (CHAN, "b", "co", "yh")]).astype(jnp.int32)

    half, both_halves = group // 2, 2 * part
    whole = [pltpu.VMEM((4 * across, piece, width), BF16)] * 2 + [pltpu.SemaphoreType.DMA((8,))]
    both, sig_t, cols = pl.pallas_call(
        functools.partial(first_kernel, n),
        out_shape=(
            struct((half, 4 * rows, lanes), BF16),
            struct((2, both_halves, lanes), BF16),
            struct((2, lanes, part), BF16),
        ),
        in_specs=[SMEM] + [ANY] * 6 + [VMEM] * 2,
        out_specs=(VMEM,) * 3,
        scratch_shapes=[
            pltpu.VMEM((half, 4 * rows, lanes), F32),
            pltpu.VMEM((4, lanes, part), F32),
            pltpu.VMEM((2, lanes, width), BF16),
        ]
        + whole,
        compiler_params=PARAMS,
        name="first",
    )(at, *blocks, cross, in_hbm(acts), in_hbm(pal))
    turned = lax.all_to_all(both, TURN, split_axis=0, concat_axis=0, tiled=True)
    parts, kept, ahead_out, behind_out = pl.pallas_call(
        functools.partial(second_kernel, n),
        out_shape=(pltpu.HBM((half, 2 * rows, part), BF16), struct((2, n, both_halves), BF16))
        + (struct((n, both_halves), BF16),) * 2,
        in_specs=[SMEM] + [VMEM] * 3,
        out_specs=(VMEM,) * 4,
        scratch_shapes=[
            pltpu.VMEM((half * 4 * rows, lanes), F32),
            pltpu.VMEM((2, both_halves, lanes), F32),
            pltpu.VMEM((half, 2 * rows, part), F32),
            pltpu.VMEM((2, n, both_halves), F32),
        ],
        compiler_params=PARAMS,
        name="second",
    )(at, turned, sig_t, cols)
    ahead_in = lax.ppermute(ahead_out, "b", SWAP)
    behind_in = lax.ppermute(behind_out, "co", SWAP)
    terms = lax.all_to_all(parts, TURN, split_axis=0, concat_axis=0, tiled=True)
    mixed, gate_grad, signal_grad = pl.pallas_call(
        third_kernel,
        out_shape=(struct(signal.shape, BF16),) * 3,
        in_specs=[SMEM] + [VMEM] * 5 + [ANY] * 6,
        out_specs=(VMEM,) * 3,
        scratch_shapes=[pltpu.VMEM((4, n, part), BF16)] * 2 + whole,
        compiler_params=PARAMS,
        cost_estimate=pl.CostEstimate(flops=10**9, bytes_accessed=6 * 2**20, transcendentals=0),
        name="third",
    )(at, kept, ahead_in, behind_in, gate, cotangent, *blocks, in_hbm(cross))
    grads = jnp.sum(terms.astype(F32), axis=0)
    return (mixed, grads[rows:].T, grads[:rows].T, gate_grad, signal_grad)


def solution(mesh):
    split = Mesh(mesh.devices.reshape(2, 2, 4, 4, 2, 2, 2), SEQ + CHAN)
    rows = P(CHAN, SEQ, None)
    return jax.shard_map(
        local,
        mesh=split,
        in_specs=(rows, P(CHAN, None), P(CHAN, None), rows, rows),
        out_specs=(rows, P(CHAN, SEQ), P(CHAN, SEQ), rows, rows),
        check_vma=False,
    )
```

```python
import functools

import jax
import jax.numpy as jnp
from jax import lax
from jax.experimental import pallas as pl
from jax.experimental.pallas import tpu as pltpu
from jax.sharding import Mesh, PartitionSpec as P

SWAP = [(0, 1), (1, 0)]
SEQ = ("h", "b", "x", "zh", "zl")
TURN = ("h", "x", "zh", "zl")
SPREAD = ("x", "zl")
CHAN = ("yh", "co")
F32, BF16 = jnp.float32, jnp.bfloat16
PARAMS = pltpu.CompilerParams(vmem_limit_bytes=24 * 2**20)
VMEM = pl.BlockSpec(memory_space=pltpu.VMEM)
SMEM = pl.BlockSpec(memory_space=pltpu.SMEM)
ANY = pl.BlockSpec(memory_space=pl.ANY)


def dot(a, b, dims=((1,), (0,))):
    return lax.dot_general(a, b, (dims, ((), ())), preferred_element_type=F32)


def assemble(q, blocks, right_ref, left_ref, sems):
    count = right_ref.shape[0] // 4
    piece = right_ref.shape[1]
    own_right, own_left, near_right, near_left, far, cross = blocks
    sources = (
        (own_right, own_left),
        (near_right, near_left),
        (far.at[:, :piece], far.at[:, piece:]),
        (cross.at[:, :piece], cross.at[:, piece:]),
    )
    copies = []
    for r, pair in enumerate(sources):
        for f, (source, target) in enumerate(zip(pair, (right_ref, left_ref))):
            to = target.at[pl.ds((q ^ r) * count, count)]
            copies.append(pltpu.make_async_copy(source, to, sems.at[2 * r + f]))
    for copy in copies:
        copy.start()
    return copies


def one_hot(rows, columns, target):
    row = lax.broadcasted_iota(jnp.int32, (rows, columns), 0)
    column = lax.broadcasted_iota(jnp.int32, (rows, columns), 1)
    return jnp.where(column == target(row), 1.0, 0.0).astype(BF16)


def activations_kernel(n, at_ref, mine_ref, near_ref, here_ref, grads_ref, sig_t_ref, cols_ref, held, used):
    q, b, co = at_ref[0], at_ref[1], at_ref[2]
    rows = here_ref.shape[0] // 16
    chans = n // rows
    part = cols_ref.shape[2]
    perm = one_hot(4 * n, 4 * n, lambda o: o // chans % 4 * n + o % chans * rows + o // (4 * chans))
    for other in range(2):
        slot = b ^ other
        starts = [4 * n * other + 2 * n * far for far in range(2)]
        sig = [ref[at : at + n] for at in starts for ref in (mine_ref, near_ref)]
        grad = [ref[at + n : at + 2 * n] for at in starts for ref in (mine_ref, near_ref)]
        sig = dot(perm, jnp.concatenate(sig, axis=0))
        grad = dot(perm, jnp.concatenate(grad, axis=0))
        for a in range(4):
            held[a] = sig[:, a * part : (a + 1) * part]
        sig_t_ref[slot, :part, :] = held[b].T.astype(BF16)
        sig_t_ref[slot, part:, :] = held[2 + b].T.astype(BF16)
        for a in range(4):
            held[a] = grad[:, a * part : (a + 1) * part]
        cols_ref[slot] = held[q].astype(BF16)
        used[slot] = grad.astype(BF16)
        if other == 0:
            here_ref[...] = sig.astype(BF16)
    grads_ref[...] = used[co]


def first_kernel(at_ref, *refs):
    blocks, (here_ref, grads_ref, both_ref, out, right_ref, left_ref, sems) = refs[:6], refs[6:]
    copies = assemble(at_ref[0], blocks, right_ref, left_ref, sems)
    lanes, width = here_ref.shape
    part = width // 4
    rows = both_ref.shape[1] // 4
    for copy in copies:
        copy.wait()
    inner = dot(right_ref[...].reshape(width, width), here_ref[...], ((1,), (1,)))
    turned = dot(grads_ref[...], left_ref[...].reshape(width, width)).T
    group = part // rows
    for h in range(2):
        for c in range(2):
            at = (2 * h + c) * part
            block = inner[at : at + part].reshape(group, rows, lanes)
            out[h * group : (h + 1) * group, c * rows : (c + 1) * rows, :] = block
            block = turned[at : at + part].reshape(group, rows, lanes)
            out[h * group : (h + 1) * group, (2 + c) * rows : (3 + c) * rows, :] = block
    both_ref[...] = out[...].astype(BF16)


def second_kernel(n, at_ref, turned_ref, sig_t_ref, cols_ref, *refs):
    parts_ref, kept_ref, ahead_out_ref, behind_out_ref, held, swapped, out, picked = refs
    b, yh = at_ref[1], at_ref[3]
    group, count, lanes = turned_ref.shape
    rows = count // 4
    part = cols_ref.shape[2]
    wide = lanes // rows
    chans = n // rows
    pick = [one_hot(n, lanes, lambda m: m % rows * 4 * chans + r * chans + m // rows) for r in range(2)]
    held[...] = turned_ref[...].astype(F32).reshape(group * count, lanes)
    block = lax.broadcasted_iota(jnp.int32, (group, lanes), 1) // wide
    for half in range(2):
        for c in range(2):
            first = (2 * half + c) * rows
            pieces = [held[pl.ds(first + k, group, stride=count), :] for k in range(rows)]
            for i in range(rows):
                acc = pieces[i]
                for k in range(rows):
                    if k != i:
                        acc = jnp.where(block == k, pltpu.roll(pieces[k], (k - i) % rows * wide, 1), acc)
                swapped[c, pl.ds(i, group, stride=rows), :] = acc
        if half == 0:
            total = 0.0
            for c in range(2):
                moved = swapped[c].astype(BF16)
                total += dot(moved, cols_ref[c])
                picked[c] = dot(pick[0], moved, ((1,), (1,)))
            out[:, :rows, :] = total.reshape(group, rows, part)
            kept_ref[0] = picked[b].astype(BF16)
            ahead_out_ref[...] = picked[1 - b].astype(BF16)
        else:
            total = 0.0
            for c in range(2):
                mine = swapped[c, pl.ds(pl.multiple_of(yh * part, part), part), :].T.astype(BF16)
                total += dot(sig_t_ref[c], mine)
            out[:, rows:, :] = total.reshape(group, rows, part)
            moved = swapped[b].astype(BF16)
            kept_ref[1] = dot(pick[0], moved, ((1,), (1,))).astype(BF16)
            behind_out_ref[...] = dot(pick[1], moved, ((1,), (1,))).astype(BF16)
    parts_ref[...] = out[...].astype(BF16)


def third_kernel(at_ref, kept_ref, ahead_in_ref, behind_in_ref, gate_ref, cot_ref, *refs):
    blocks, refs = refs[:6], refs[6:]
    mixed_ref, gate_grad_ref, signal_grad_ref, ahead, behind, right_ref, left_ref, sems = refs
    b, co = at_ref[1], at_ref[2]
    copies = assemble(at_ref[0], blocks, right_ref, left_ref, sems)
    shape = gate_ref.shape
    part = ahead.shape[2]
    for h in range(2):
        at = slice(h * part, (h + 1) * part)
        ahead[2 * h + b] = kept_ref[0, :, at]
        ahead[2 * h + 1 - b] = ahead_in_ref[:, at]
        behind[2 * h + co] = kept_ref[1, :, at]
        behind[2 * h + 1 - co] = behind_in_ref[:, at]
    width = shape[2]
    for copy in copies:
        copy.wait()
    every = jnp.concatenate([ahead[a] for a in range(4)], axis=1)
    value = dot(every, left_ref[...].reshape(width, width), ((1,), (1,))).reshape(shape)
    mixed_ref[...] = (gate_ref[...].astype(F32) * value).astype(BF16)
    gate_grad_ref[...] = (cot_ref[...].astype(F32) * value).astype(BF16)
    every = jnp.concatenate([behind[a] for a in range(4)], axis=1)
    signal_grad_ref[...] = dot(every, right_ref[...].reshape(width, width)).reshape(shape).astype(BF16)


def local(signal, right_factor, left_factor, gate, cotangent):
    chans, rows, width = signal.shape
    part = right_factor.shape[0]
    group, n = width // rows, chans * rows
    lanes = 4 * n
    struct = jax.ShapeDtypeStruct
    low = lax.axis_size(("h", "b"))
    count = 2 * low
    mirror = []
    for y in range(count):
        t = count - 1 - y
        mirror.append(((y % low) * 2 + y // low, (t % low) * 2 + t // low))
    across = lax.axis_size(SPREAD)
    piece = part // across
    start = lax.axis_index(SPREAD) * piece
    value_grad = (gate.astype(F32) * cotangent.astype(F32)).astype(BF16)
    sv = jnp.concatenate([signal.reshape(n, width), value_grad.reshape(n, width)], axis=0)
    mine = jnp.concatenate(
        [lax.dynamic_slice_in_dim(f, start, piece, axis=0) for f in (right_factor, left_factor)], axis=0
    )
    far_mine = lax.ppermute(mine, ("h", "b", "yh"), mirror)
    far_sv = lax.ppermute(sv, "yh", SWAP)
    far_mine, far_sv, sv, right, left = lax.optimization_barrier((far_mine, far_sv, sv, right_factor, left_factor))
    copies = jnp.broadcast_to(far_mine[None], (across,) + far_mine.shape)
    far = lax.all_to_all(copies, SPREAD, split_axis=0, concat_axis=0, tiled=True)
    half_acts = jnp.concatenate([sv, far_sv], axis=0)
    acts = jnp.concatenate([half_acts, lax.ppermute(half_acts, "b", SWAP)], axis=0)
    near_acts = lax.ppermute(acts, "co", SWAP)
    near_right, near_left = (lax.ppermute(f, "co", SWAP) for f in (right, left))
    at = jnp.stack([lax.axis_index(a) for a in (CHAN, "b", "co", "yh")]).astype(jnp.int32)
    half, both_halves = group // 2, 2 * part
    prepared = pl.pallas_call(
        functools.partial(activations_kernel, n),
        out_shape=(
            struct((lanes, width), BF16),
            struct((lanes, width), BF16),
            struct((2, both_halves, lanes), BF16),
            struct((2, lanes, part), BF16),
        ),
        in_specs=[SMEM] + [VMEM] * 2,
        out_specs=(VMEM,) * 4,
        scratch_shapes=[pltpu.VMEM((4, lanes, part), F32), pltpu.VMEM((2, lanes, width), BF16)],
        compiler_params=PARAMS,
        cost_estimate=pl.CostEstimate(flops=10**8, bytes_accessed=2 * 2**20, transcendentals=0),
        name="activations",
    )(at, acts, near_acts)
    far, prepared, near_right, near_left = lax.optimization_barrier((far, prepared, near_right, near_left))
    here, grads_here, sig_t, cols = prepared
    cross = lax.ppermute(far, "co", SWAP)
    in_hbm = functools.partial(pltpu.with_memory_space_constraint, memory_space=pltpu.HBM)
    near = [f.reshape(across, piece, width) for f in (right_factor, left_factor, near_right, near_left)]
    blocks = [in_hbm(f) for f in (*near, far)]

    whole = [pltpu.VMEM((4 * across, piece, width), BF16)] * 2 + [pltpu.SemaphoreType.DMA((8,))]
    both = pl.pallas_call(
        first_kernel,
        out_shape=struct((half, 4 * rows, lanes), BF16),
        in_specs=[SMEM] + [ANY] * 6 + [VMEM] * 2,
        out_specs=VMEM,
        scratch_shapes=[pltpu.VMEM((half, 4 * rows, lanes), F32)] + whole,
        compiler_params=PARAMS,
        name="first",
    )(at, *blocks, cross, here, grads_here)
    turned = lax.all_to_all(both, TURN, split_axis=0, concat_axis=0, tiled=True)
    parts, kept, ahead_out, behind_out = pl.pallas_call(
        functools.partial(second_kernel, n),
        out_shape=(pltpu.HBM((half, 2 * rows, part), BF16), struct((2, n, both_halves), BF16))
        + (struct((n, both_halves), BF16),) * 2,
        in_specs=[SMEM] + [VMEM] * 3,
        out_specs=(VMEM,) * 4,
        scratch_shapes=[
            pltpu.VMEM((half * 4 * rows, lanes), F32),
            pltpu.VMEM((2, both_halves, lanes), F32),
            pltpu.VMEM((half, 2 * rows, part), F32),
            pltpu.VMEM((2, n, both_halves), F32),
        ],
        compiler_params=PARAMS,
        name="second",
    )(at, turned, sig_t, cols)
    ahead_in = lax.ppermute(ahead_out, "b", SWAP)
    behind_in = lax.ppermute(behind_out, "co", SWAP)
    terms = lax.all_to_all(parts, TURN, split_axis=0, concat_axis=0, tiled=True)
    mixed, gate_grad, signal_grad = pl.pallas_call(
        third_kernel,
        out_shape=(struct(signal.shape, BF16),) * 3,
        in_specs=[SMEM] + [VMEM] * 5 + [ANY] * 6,
        out_specs=(VMEM,) * 3,
        scratch_shapes=[pltpu.VMEM((4, n, part), BF16)] * 2 + whole,
        compiler_params=PARAMS,
        cost_estimate=pl.CostEstimate(flops=10**9, bytes_accessed=6 * 2**20, transcendentals=0),
        name="third",
    )(at, kept, ahead_in, behind_in, gate, cotangent, *blocks, in_hbm(cross))
    grads = jnp.sum(terms.astype(F32), axis=0)
    return (mixed, grads[rows:].T, grads[:rows].T, gate_grad, signal_grad)


def solution(mesh):
    split = Mesh(mesh.devices.reshape(2, 2, 4, 4, 2, 2, 2), SEQ + CHAN)
    rows = P(CHAN, SEQ, None)
    return jax.shard_map(
        local,
        mesh=split,
        in_specs=(rows, P(CHAN, None), P(CHAN, None), rows, rows),
        out_specs=(rows, P(CHAN, SEQ), P(CHAN, SEQ), rows, rows),
        check_vma=False,
    )
```

```python
import functools

import jax
import jax.numpy as jnp
from jax import lax
from jax.experimental import pallas as pl
from jax.experimental.pallas import tpu as pltpu
from jax.sharding import Mesh, PartitionSpec as P

SWAP = [(0, 1), (1, 0)]
SEQ = ("h", "b", "x", "zh", "zl")
TURN = ("h", "x", "zh", "zl")
SPREAD = ("x", "zl")
CHAN = ("yh", "co")
F32, BF16 = jnp.float32, jnp.bfloat16
PARAMS = pltpu.CompilerParams(vmem_limit_bytes=24 * 2**20)
VMEM = pl.BlockSpec(memory_space=pltpu.VMEM)
SMEM = pl.BlockSpec(memory_space=pltpu.SMEM)
ANY = pl.BlockSpec(memory_space=pl.ANY)


def dot(a, b, dims=((1,), (0,))):
    return lax.dot_general(a, b, (dims, ((), ())), preferred_element_type=F32)


def assemble(q, blocks, right_ref, left_ref, sems):
    count = right_ref.shape[0] // 4
    piece = right_ref.shape[1]
    own_right, own_left, near, far, cross = blocks
    base = near.shape[0] - 2 * count
    sources = (
        (own_right, own_left),
        (near.at[base : base + count], near.at[base + count :]),
        (far.at[:, :piece], far.at[:, piece:]),
        (cross.at[:, :piece], cross.at[:, piece:]),
    )
    copies = []
    for f, target in enumerate((right_ref, left_ref)):
        for r, pair in enumerate(sources):
            to = target.at[pl.ds((q ^ r) * count, count)]
            copies.append(pltpu.make_async_copy(pair[f], to, sems.at[4 * f + r]))
    for copy in copies:
        copy.start()
    return copies


def one_hot(rows, columns, target):
    row = lax.broadcasted_iota(jnp.int32, (rows, columns), 0)
    column = lax.broadcasted_iota(jnp.int32, (rows, columns), 1)
    return jnp.where(column == target(row), 1.0, 0.0).astype(BF16)


def activations_kernel(n, at_ref, mine_ref, near_ref, here_ref, grads_ref, sig_t_ref, cols_ref, held, used):
    q, b, co = at_ref[0], at_ref[1], at_ref[2]
    rows = here_ref.shape[0] // 16
    chans = n // rows
    part = cols_ref.shape[2]
    perm = one_hot(4 * n, 4 * n, lambda o: o // chans % 4 * n + o % chans * rows + o // (4 * chans))
    for other in range(2):
        slot = b ^ other
        starts = [4 * n * other + 2 * n * far for far in range(2)]
        sig = [ref[at : at + n] for at in starts for ref in (mine_ref, near_ref)]
        grad = [ref[at + n : at + 2 * n] for at in starts for ref in (mine_ref, near_ref)]
        sig = dot(perm, jnp.concatenate(sig, axis=0))
        grad = dot(perm, jnp.concatenate(grad, axis=0))
        for a in range(4):
            held[a] = sig[:, a * part : (a + 1) * part]
        sig_t_ref[slot, :part, :] = held[b].T.astype(BF16)
        sig_t_ref[slot, part:, :] = held[2 + b].T.astype(BF16)
        for a in range(4):
            held[a] = grad[:, a * part : (a + 1) * part]
        cols_ref[slot] = held[q].astype(BF16)
        used[slot] = grad.astype(BF16)
        if other == 0:
            here_ref[...] = sig.astype(BF16)
    grads_ref[...] = used[co]


def first_kernel(at_ref, *refs):
    blocks, (here_ref, grads_ref, both_ref, out, right_ref, left_ref, sems) = refs[:5], refs[5:]
    copies = assemble(at_ref[0], blocks, right_ref, left_ref, sems)
    lanes, width = here_ref.shape
    part = width // 4
    rows = both_ref.shape[1] // 4
    for copy in copies[:4]:
        copy.wait()
    inner = dot(right_ref[...].reshape(width, width), here_ref[...], ((1,), (1,)))
    for copy in copies[4:]:
        copy.wait()
    turned = dot(grads_ref[...], left_ref[...].reshape(width, width)).T
    group = part // rows
    for h in range(2):
        for c in range(2):
            at = (2 * h + c) * part
            block = inner[at : at + part].reshape(group, rows, lanes)
            out[h * group : (h + 1) * group, c * rows : (c + 1) * rows, :] = block
            block = turned[at : at + part].reshape(group, rows, lanes)
            out[h * group : (h + 1) * group, (2 + c) * rows : (3 + c) * rows, :] = block
    both_ref[...] = out[...].astype(BF16)


def second_kernel(n, at_ref, turned_ref, sig_t_ref, cols_ref, *refs):
    parts_ref, kept_ref, ahead_out_ref, behind_out_ref, held, swapped, out, picked = refs
    b, yh = at_ref[1], at_ref[3]
    group, count, lanes = turned_ref.shape
    rows = count // 4
    part = cols_ref.shape[2]
    wide = lanes // rows
    chans = n // rows
    pick = [one_hot(n, lanes, lambda m: m % rows * 4 * chans + r * chans + m // rows) for r in range(2)]
    held[...] = turned_ref[...].astype(F32).reshape(group * count, lanes)
    block = lax.broadcasted_iota(jnp.int32, (group, lanes), 1) // wide
    for half in range(2):
        for c in range(2):
            first = (2 * half + c) * rows
            pieces = [held[pl.ds(first + k, group, stride=count), :] for k in range(rows)]
            for i in range(rows):
                acc = pieces[i]
                for k in range(rows):
                    if k != i:
                        acc = jnp.where(block == k, pltpu.roll(pieces[k], (k - i) % rows * wide, 1), acc)
                swapped[c, pl.ds(i, group, stride=rows), :] = acc
        if half == 0:
            total = 0.0
            for c in range(2):
                moved = swapped[c].astype(BF16)
                total += dot(moved, cols_ref[c])
                picked[c] = dot(pick[0], moved, ((1,), (1,)))
            out[:, :rows, :] = total.reshape(group, rows, part)
            kept_ref[0] = picked[b].astype(BF16)
            ahead_out_ref[...] = picked[1 - b].astype(BF16)
        else:
            total = 0.0
            for c in range(2):
                mine = swapped[c, pl.ds(pl.multiple_of(yh * part, part), part), :].T.astype(BF16)
                total += dot(sig_t_ref[c], mine)
            out[:, rows:, :] = total.reshape(group, rows, part)
            moved = swapped[b].astype(BF16)
            kept_ref[1] = dot(pick[0], moved, ((1,), (1,))).astype(BF16)
            behind_out_ref[...] = dot(pick[1], moved, ((1,), (1,))).astype(BF16)
    parts_ref[...] = out[...].astype(BF16)


def third_kernel(at_ref, kept_ref, ahead_in_ref, behind_in_ref, gate_ref, cot_ref, *refs):
    blocks, refs = refs[:5], refs[5:]
    mixed_ref, gate_grad_ref, signal_grad_ref, ahead, behind, right_ref, left_ref, sems = refs
    b, co = at_ref[1], at_ref[2]
    copies = assemble(at_ref[0], blocks, right_ref, left_ref, sems)
    shape = gate_ref.shape
    part = ahead.shape[2]
    for h in range(2):
        at = slice(h * part, (h + 1) * part)
        ahead[2 * h + b] = kept_ref[0, :, at]
        ahead[2 * h + 1 - b] = ahead_in_ref[:, at]
        behind[2 * h + co] = kept_ref[1, :, at]
        behind[2 * h + 1 - co] = behind_in_ref[:, at]
    width = shape[2]
    for copy in copies:
        copy.wait()
    every = jnp.concatenate([ahead[a] for a in range(4)], axis=1)
    value = dot(every, left_ref[...].reshape(width, width), ((1,), (1,))).reshape(shape)
    mixed_ref[...] = (gate_ref[...].astype(F32) * value).astype(BF16)
    gate_grad_ref[...] = (cot_ref[...].astype(F32) * value).astype(BF16)
    every = jnp.concatenate([behind[a] for a in range(4)], axis=1)
    signal_grad_ref[...] = dot(every, right_ref[...].reshape(width, width)).reshape(shape).astype(BF16)


def local(signal, right_factor, left_factor, gate, cotangent):
    chans, rows, width = signal.shape
    part = right_factor.shape[0]
    group, n = width // rows, chans * rows
    lanes = 4 * n
    struct = jax.ShapeDtypeStruct
    low = lax.axis_size(("h", "b"))
    count = 2 * low
    mirror = []
    for y in range(count):
        t = count - 1 - y
        mirror.append(((y % low) * 2 + y // low, (t % low) * 2 + t // low))
    across = lax.axis_size(SPREAD)
    piece = part // across
    start = lax.axis_index(SPREAD) * piece
    value_grad = (gate.astype(F32) * cotangent.astype(F32)).astype(BF16)
    sv = jnp.concatenate([signal.reshape(n, width), value_grad.reshape(n, width)], axis=0)
    mine = jnp.concatenate(
        [lax.dynamic_slice_in_dim(f, start, piece, axis=0) for f in (right_factor, left_factor)], axis=0
    )
    far_mine = lax.ppermute(mine, ("h", "b", "yh"), mirror)
    far_sv = lax.ppermute(sv, "yh", SWAP)
    far_mine, far_sv, sv, right, left = lax.optimization_barrier((far_mine, far_sv, sv, right_factor, left_factor))
    copies = jnp.broadcast_to(far_mine[None], (across,) + far_mine.shape)
    far = lax.all_to_all(copies, SPREAD, split_axis=0, concat_axis=0, tiled=True)
    half_acts = jnp.concatenate([sv, far_sv], axis=0)
    acts = jnp.concatenate([half_acts, lax.ppermute(half_acts, "b", SWAP)], axis=0)
    near_all = lax.ppermute(jnp.concatenate([acts, right, left], axis=0), "co", SWAP)
    near_acts = near_all[: 8 * n]
    at = jnp.stack([lax.axis_index(a) for a in (CHAN, "b", "co", "yh")]).astype(jnp.int32)
    half, both_halves = group // 2, 2 * part
    prepared = pl.pallas_call(
        functools.partial(activations_kernel, n),
        out_shape=(
            struct((lanes, width), BF16),
            struct((lanes, width), BF16),
            struct((2, both_halves, lanes), BF16),
            struct((2, lanes, part), BF16),
        ),
        in_specs=[SMEM] + [VMEM] * 2,
        out_specs=(VMEM,) * 4,
        scratch_shapes=[pltpu.VMEM((4, lanes, part), F32), pltpu.VMEM((2, lanes, width), BF16)],
        compiler_params=PARAMS,
        cost_estimate=pl.CostEstimate(flops=10**8, bytes_accessed=2 * 2**20, transcendentals=0),
        name="activations",
    )(at, acts, near_acts)
    far, prepared, near_all = lax.optimization_barrier((far, prepared, near_all))
    here, grads_here, sig_t, cols = prepared
    cross = lax.ppermute(far, "co", SWAP)
    in_hbm = functools.partial(pltpu.with_memory_space_constraint, memory_space=pltpu.HBM)
    near = [f.reshape(-1, piece, width) for f in (right_factor, left_factor, near_all)]
    blocks = [in_hbm(f) for f in (*near, far)]

    whole = [pltpu.VMEM((4 * across, piece, width), BF16)] * 2 + [pltpu.SemaphoreType.DMA((8,))]
    both = pl.pallas_call(
        first_kernel,
        out_shape=struct((half, 4 * rows, lanes), BF16),
        in_specs=[SMEM] + [ANY] * 5 + [VMEM] * 2,
        out_specs=VMEM,
        scratch_shapes=[pltpu.VMEM((half, 4 * rows, lanes), F32)] + whole,
        compiler_params=PARAMS,
        name="first",
    )(at, *blocks, cross, here, grads_here)
    turned = lax.all_to_all(both, TURN, split_axis=0, concat_axis=0, tiled=True)
    parts, kept, ahead_out, behind_out = pl.pallas_call(
        functools.partial(second_kernel, n),
        out_shape=(pltpu.HBM((half, 2 * rows, part), BF16), struct((2, n, both_halves), BF16))
        + (struct((n, both_halves), BF16),) * 2,
        in_specs=[SMEM] + [VMEM] * 3,
        out_specs=(VMEM,) * 4,
        scratch_shapes=[
            pltpu.VMEM((half * 4 * rows, lanes), F32),
            pltpu.VMEM((2, both_halves, lanes), F32),
            pltpu.VMEM((half, 2 * rows, part), F32),
            pltpu.VMEM((2, n, both_halves), F32),
        ],
        compiler_params=PARAMS,
        name="second",
    )(at, turned, sig_t, cols)
    ahead_in = lax.ppermute(ahead_out, "b", SWAP)
    behind_in = lax.ppermute(behind_out, "co", SWAP)
    terms = lax.all_to_all(parts, TURN, split_axis=0, concat_axis=0, tiled=True)
    mixed, gate_grad, signal_grad = pl.pallas_call(
        third_kernel,
        out_shape=(struct(signal.shape, BF16),) * 3,
        in_specs=[SMEM] + [VMEM] * 5 + [ANY] * 5,
        out_specs=(VMEM,) * 3,
        scratch_shapes=[pltpu.VMEM((4, n, part), BF16)] * 2 + whole,
        compiler_params=PARAMS,
        cost_estimate=pl.CostEstimate(flops=10**9, bytes_accessed=6 * 2**20, transcendentals=0),
        name="third",
    )(at, kept, ahead_in, behind_in, gate, cotangent, *blocks, in_hbm(cross))
    grads = jnp.sum(terms.astype(F32), axis=0)
    return (mixed, grads[rows:].T, grads[:rows].T, gate_grad, signal_grad)


def solution(mesh):
    split = Mesh(mesh.devices.reshape(2, 2, 4, 4, 2, 2, 2), SEQ + CHAN)
    rows = P(CHAN, SEQ, None)
    return jax.shard_map(
        local,
        mesh=split,
        in_specs=(rows, P(CHAN, None), P(CHAN, None), rows, rows),
        out_specs=(rows, P(CHAN, SEQ), P(CHAN, SEQ), rows, rows),
        check_vma=False,
    )
```

```python
import functools

import jax
import jax.numpy as jnp
from jax import lax
from jax.experimental import pallas as pl
from jax.experimental.pallas import tpu as pltpu
from jax.sharding import Mesh, PartitionSpec as P

SWAP = [(0, 1), (1, 0)]
SEQ = ("h", "b", "x", "zh", "zl")
TURN = ("h", "x", "zh", "zl")
SPREAD = ("x", "zl")
CHAN = ("yh", "co")
F32, BF16 = jnp.float32, jnp.bfloat16
PARAMS = pltpu.CompilerParams(vmem_limit_bytes=24 * 2**20)
VMEM = pl.BlockSpec(memory_space=pltpu.VMEM)
SMEM = pl.BlockSpec(memory_space=pltpu.SMEM)
ANY = pl.BlockSpec(memory_space=pl.ANY)


def dot(a, b, dims=((1,), (0,))):
    return lax.dot_general(a, b, (dims, ((), ())), preferred_element_type=F32)


def assemble(q, blocks, right_ref, left_ref, sems):
    count = right_ref.shape[0] // 4
    piece = right_ref.shape[1]
    own_right, own_left, near, far, cross = blocks
    base = near.shape[0] - 2 * count
    sources = (
        (own_right, own_left),
        (near.at[base : base + count], near.at[base + count :]),
        (far.at[:, :piece], far.at[:, piece:]),
        (cross.at[:, :piece], cross.at[:, piece:]),
    )
    copies = []
    for f, target in enumerate((right_ref, left_ref)):
        for r, pair in enumerate(sources):
            to = target.at[pl.ds((q ^ r) * count, count)]
            copies.append(pltpu.make_async_copy(pair[f], to, sems.at[4 * f + r]))
    for copy in copies:
        copy.start()
    return copies


def one_hot(rows, columns, target):
    row = lax.broadcasted_iota(jnp.int32, (rows, columns), 0)
    column = lax.broadcasted_iota(jnp.int32, (rows, columns), 1)
    return jnp.where(column == target(row), 1.0, 0.0).astype(BF16)


def activations_kernel(n, at_ref, mine_ref, near_ref, here_ref, grads_ref, sig_t_ref, cols_ref, held, used):
    q, b, co = at_ref[0], at_ref[1], at_ref[2]
    rows = here_ref.shape[0] // 16
    chans = n // rows
    part = cols_ref.shape[2]
    perm = one_hot(4 * n, 4 * n, lambda o: o // chans % 4 * n + o % chans * rows + o // (4 * chans))
    for other in range(2):
        slot = b ^ other
        starts = [4 * n * other + 2 * n * far for far in range(2)]
        sig = [ref[at : at + n] for at in starts for ref in (mine_ref, near_ref)]
        grad = [ref[at + n : at + 2 * n] for at in starts for ref in (mine_ref, near_ref)]
        sig = dot(perm, jnp.concatenate(sig, axis=0))
        grad = dot(perm, jnp.concatenate(grad, axis=0))
        for a in range(4):
            held[a] = sig[:, a * part : (a + 1) * part]
        sig_t_ref[slot, :part, :] = held[b].T.astype(BF16)
        sig_t_ref[slot, part:, :] = held[2 + b].T.astype(BF16)
        for a in range(4):
            held[a] = grad[:, a * part : (a + 1) * part]
        cols_ref[slot] = held[q].astype(BF16)
        used[slot] = grad.astype(BF16)
        if other == 0:
            here_ref[...] = sig.astype(BF16)
    grads_ref[...] = used[co]


def first_kernel(at_ref, *refs):
    blocks, (here_ref, grads_ref, both_ref, out, right_ref, left_ref, sems) = refs[:5], refs[5:]
    copies = assemble(at_ref[0], blocks, right_ref, left_ref, sems)
    lanes, width = here_ref.shape
    part = width // 4
    rows = both_ref.shape[1] // 4
    for copy in copies[:4]:
        copy.wait()
    inner = dot(right_ref[...].reshape(width, width), here_ref[...], ((1,), (1,)))
    for copy in copies[4:]:
        copy.wait()
    turned = dot(grads_ref[...], left_ref[...].reshape(width, width)).T
    group = part // rows
    for h in range(2):
        for c in range(2):
            at = (2 * h + c) * part
            block = inner[at : at + part].reshape(group, rows, lanes)
            out[h * group : (h + 1) * group, c * rows : (c + 1) * rows, :] = block
            block = turned[at : at + part].reshape(group, rows, lanes)
            out[h * group : (h + 1) * group, (2 + c) * rows : (3 + c) * rows, :] = block
    both_ref[...] = out[...].astype(BF16)


def second_kernel(n, at_ref, turned_ref, sig_t_ref, cols_ref, *refs):
    parts_ref, kept_ref, ahead_out_ref, behind_out_ref, held, swapped, picked = refs
    b, yh = at_ref[1], at_ref[3]
    group, count, lanes = turned_ref.shape
    rows = count // 4
    part = cols_ref.shape[2]
    wide = lanes // rows
    chans = n // rows
    pick = [one_hot(n, lanes, lambda m: m % rows * 4 * chans + r * chans + m // rows) for r in range(2)]
    held[...] = turned_ref[...].astype(F32).reshape(group * count, lanes)
    block = lax.broadcasted_iota(jnp.int32, (group, lanes), 1) // wide
    for half in range(2):
        for c in range(2):
            first = (2 * half + c) * rows
            pieces = [held[pl.ds(first + k, group, stride=count), :] for k in range(rows)]
            for i in range(rows):
                acc = pieces[i]
                for k in range(rows):
                    if k != i:
                        acc = jnp.where(block == k, pltpu.roll(pieces[k], (k - i) % rows * wide, 1), acc)
                swapped[c, pl.ds(i, group, stride=rows), :] = acc
        if half == 0:
            total = 0.0
            for c in range(2):
                moved = swapped[c].astype(BF16)
                total += dot(moved, cols_ref[c])
                picked[c] = dot(pick[0], moved, ((1,), (1,)))
            left = total.reshape(group, rows, part)
            kept_ref[0] = picked[b].astype(BF16)
            ahead_out_ref[...] = picked[1 - b].astype(BF16)
        else:
            total = 0.0
            for c in range(2):
                mine = swapped[c, pl.ds(pl.multiple_of(yh * part, part), part), :].T.astype(BF16)
                total += dot(sig_t_ref[c], mine)
            right = total.reshape(group, rows, part)
            moved = swapped[b].astype(BF16)
            kept_ref[1] = dot(pick[0], moved, ((1,), (1,))).astype(BF16)
            behind_out_ref[...] = dot(pick[1], moved, ((1,), (1,))).astype(BF16)
    parts_ref[...] = jnp.concatenate([left, right], axis=1).astype(BF16)


def third_kernel(at_ref, kept_ref, ahead_in_ref, behind_in_ref, gate_ref, cot_ref, *refs):
    blocks, refs = refs[:5], refs[5:]
    mixed_ref, gate_grad_ref, signal_grad_ref, ahead, behind, right_ref, left_ref, sems = refs
    b, co = at_ref[1], at_ref[2]
    copies = assemble(at_ref[0], blocks, right_ref, left_ref, sems)
    shape = gate_ref.shape
    part = ahead.shape[2]
    for h in range(2):
        at = slice(h * part, (h + 1) * part)
        ahead[2 * h + b] = kept_ref[0, :, at]
        ahead[2 * h + 1 - b] = ahead_in_ref[:, at]
        behind[2 * h + co] = kept_ref[1, :, at]
        behind[2 * h + 1 - co] = behind_in_ref[:, at]
    width = shape[2]
    for copy in copies:
        copy.wait()
    every = jnp.concatenate([ahead[a] for a in range(4)], axis=1)
    value = dot(every, left_ref[...].reshape(width, width), ((1,), (1,))).reshape(shape)
    mixed_ref[...] = (gate_ref[...].astype(F32) * value).astype(BF16)
    gate_grad_ref[...] = (cot_ref[...].astype(F32) * value).astype(BF16)
    every = jnp.concatenate([behind[a] for a in range(4)], axis=1)
    signal_grad_ref[...] = dot(every, right_ref[...].reshape(width, width)).reshape(shape).astype(BF16)


def local(signal, right_factor, left_factor, gate, cotangent):
    chans, rows, width = signal.shape
    part = right_factor.shape[0]
    group, n = width // rows, chans * rows
    lanes = 4 * n
    struct = jax.ShapeDtypeStruct
    low = lax.axis_size(("h", "b"))
    count = 2 * low
    mirror = []
    for y in range(count):
        t = count - 1 - y
        mirror.append(((y % low) * 2 + y // low, (t % low) * 2 + t // low))
    across = lax.axis_size(SPREAD)
    piece = part // across
    start = lax.axis_index(SPREAD) * piece
    value_grad = (gate.astype(F32) * cotangent.astype(F32)).astype(BF16)
    sv = jnp.concatenate([signal.reshape(n, width), value_grad.reshape(n, width)], axis=0)
    mine = jnp.concatenate(
        [lax.dynamic_slice_in_dim(f, start, piece, axis=0) for f in (right_factor, left_factor)], axis=0
    )
    far_mine = lax.ppermute(mine, ("h", "b", "yh"), mirror)
    far_sv = lax.ppermute(sv, "yh", SWAP)
    far_mine, far_sv, sv, right, left = lax.optimization_barrier((far_mine, far_sv, sv, right_factor, left_factor))
    copies = jnp.broadcast_to(far_mine[None], (across,) + far_mine.shape)
    far = lax.all_to_all(copies, SPREAD, split_axis=0, concat_axis=0, tiled=True)
    half_acts = jnp.concatenate([sv, far_sv], axis=0)
    acts = jnp.concatenate([half_acts, lax.ppermute(half_acts, "b", SWAP)], axis=0)
    near_all = lax.ppermute(jnp.concatenate([acts, right, left], axis=0), "co", SWAP)
    near_acts = near_all[: 8 * n]
    at = jnp.stack([lax.axis_index(a) for a in (CHAN, "b", "co", "yh")]).astype(jnp.int32)
    half, both_halves = group // 2, 2 * part
    prepared = pl.pallas_call(
        functools.partial(activations_kernel, n),
        out_shape=(
            struct((lanes, width), BF16),
            struct((lanes, width), BF16),
            struct((2, both_halves, lanes), BF16),
            struct((2, lanes, part), BF16),
        ),
        in_specs=[SMEM] + [VMEM] * 2,
        out_specs=(VMEM,) * 4,
        scratch_shapes=[pltpu.VMEM((4, lanes, part), F32), pltpu.VMEM((2, lanes, width), BF16)],
        compiler_params=PARAMS,
        cost_estimate=pl.CostEstimate(flops=10**8, bytes_accessed=2 * 2**20, transcendentals=0),
        name="activations",
    )(at, acts, near_acts)
    far, prepared, near_all = lax.optimization_barrier((far, prepared, near_all))
    here, grads_here, sig_t, cols = prepared
    cross = lax.ppermute(far, "co", SWAP)
    in_hbm = functools.partial(pltpu.with_memory_space_constraint, memory_space=pltpu.HBM)
    near = [f.reshape(-1, piece, width) for f in (right_factor, left_factor, near_all)]
    blocks = [in_hbm(f) for f in (*near, far)]

    whole = [pltpu.VMEM((4 * across, piece, width), BF16)] * 2 + [pltpu.SemaphoreType.DMA((8,))]
    both = pl.pallas_call(
        first_kernel,
        out_shape=struct((half, 4 * rows, lanes), BF16),
        in_specs=[SMEM] + [ANY] * 5 + [VMEM] * 2,
        out_specs=VMEM,
        scratch_shapes=[pltpu.VMEM((half, 4 * rows, lanes), F32)] + whole,
        compiler_params=PARAMS,
        name="first",
    )(at, *blocks, cross, here, grads_here)
    turned = lax.all_to_all(both, TURN, split_axis=0, concat_axis=0, tiled=True)
    parts, kept, ahead_out, behind_out = pl.pallas_call(
        functools.partial(second_kernel, n),
        out_shape=(pltpu.HBM((half, 2 * rows, part), BF16), struct((2, n, both_halves), BF16))
        + (struct((n, both_halves), BF16),) * 2,
        in_specs=[SMEM] + [VMEM] * 3,
        out_specs=(VMEM,) * 4,
        scratch_shapes=[
            pltpu.VMEM((half * 4 * rows, lanes), F32),
            pltpu.VMEM((2, both_halves, lanes), F32),
            pltpu.VMEM((2, n, both_halves), F32),
        ],
        compiler_params=PARAMS,
        name="second",
    )(at, turned, sig_t, cols)
    ahead_in = lax.ppermute(ahead_out, "b", SWAP)
    behind_in = lax.ppermute(behind_out, "co", SWAP)
    terms = lax.all_to_all(parts, TURN, split_axis=0, concat_axis=0, tiled=True)
    mixed, gate_grad, signal_grad = pl.pallas_call(
        third_kernel,
        out_shape=(struct(signal.shape, BF16),) * 3,
        in_specs=[SMEM] + [VMEM] * 5 + [ANY] * 5,
        out_specs=(VMEM,) * 3,
        scratch_shapes=[pltpu.VMEM((4, n, part), BF16)] * 2 + whole,
        compiler_params=PARAMS,
        cost_estimate=pl.CostEstimate(flops=10**9, bytes_accessed=6 * 2**20, transcendentals=0),
        name="third",
    )(at, kept, ahead_in, behind_in, gate, cotangent, *blocks, in_hbm(cross))
    grads = jnp.sum(terms.astype(F32), axis=0)
    return (mixed, grads[rows:].T, grads[:rows].T, gate_grad, signal_grad)


def solution(mesh):
    split = Mesh(mesh.devices.reshape(2, 2, 4, 4, 2, 2, 2), SEQ + CHAN)
    rows = P(CHAN, SEQ, None)
    return jax.shard_map(
        local,
        mesh=split,
        in_specs=(rows, P(CHAN, None), P(CHAN, None), rows, rows),
        out_specs=(rows, P(CHAN, SEQ), P(CHAN, SEQ), rows, rows),
        check_vma=False,
    )
```
